128 devices in a mesh: dev: 128 (over y, z, x, core).
Axes of the slice: x: 4, y: 4, z: 4, core: 2. Of those that a mesh axis runs over, the one named last changes fastest.
Arguments:
- upstream: bfloat16 [65536, 1024], P('dev'), may hold values from -24 to 24
- bag: int32 [65536, 8], P('dev'), may hold values from 0 to 767
- next_bag: int32 [65536, 8], P('dev'), may hold values from 0 to 511
- hot_slots: int32 [65536], P('dev'), may hold values from 0 to 8191, as said below
- evict_dest: int32 [128, 128, 2], P('dev'), may hold values from -1 to 1023, as said below
- hot_cache: float32 [65536, 128], P('dev'), may hold values from -6 to 6
- evict_cache: float32 [32768, 128], P('dev'), may hold values from -6 to 6
- hot_table: float32 [8192, 128], P('dev'), may hold values from -6 to 6
- hot_accum: float32 [8192, 128], P('dev'), may hold values from 1 to 100
- owner_table: float32 [131072, 128], P('dev'), may hold values from -6 to 6
- owner_accum: float32 [131072, 128], P('dev'), may hold values from 1 to 30
- cross_w: float32 [2, 1024, 1024], P(None, None, 'dev'), may hold values from -0.1875 to 0.1875
- cross_b: float32 [2, 1024], P(None, 'dev'), may hold values from -3 to 3
- cross_accum: float32 [2, 1024, 1024], P(None, None, 'dev'), may hold values from 10000 to 1000000
Outputs:
- next_first: bfloat16 [65536, 1024], P('dev')
- hot_new: float32 [8192, 128], P('dev')
- hot_accum_new: float32 [8192, 128], P('dev')
- owner_new: float32 [131072, 128], P('dev')
- owner_accum_new: float32 [131072, 128], P('dev')
- cross_w_new: float32 [2, 1024, 1024], P(None, None, 'dev')
- cross_b_new: float32 [2, 1024], P(None, 'dev')
The draws below stay inside these ranges and needn't reach their ends.
Inputs may be any that keep to these rules, and one draw needn't show every extreme that they name: `hot_slots`: entry d * 512 + 4 * o + k names a row of owner o's block, o * 64 to o * 64 + 63; the 4 rows of one device in one owner's block are distinct. evict_dest[o, s, k] is the row of owner o's block (0 to 1023) that receives the gradient of source s's evicted slot 2 * o + k, or -1 for an empty slot; in each (o, s) bucket the live entries come first, and some bucket is full in every draw.
All inputs are finite; a program needn't handle non-finite values.
Results may differ from the reference program's by a relative error of at most 0.0033.
The reference program's roundings to bfloat16 on the way count: a program that leaves them out, or rounds other values in their place, can miss the bound.
Values may be sent and summed in bfloat16 or wider, within the bound.
A program may use at most 128 MiB of HBM per device.

```python
import math
import jax
import jax.numpy as jnp
from jax import lax

E = 128
F = 8
D = 1024
TOK_DEV = 512
NEXT_DEV = 512
HB = 4
HOT_DEV = 64
EVB = 2
OWN_DEV = 1024
HOTC = 512
EVC = 256
HOT = 8192
OWNED = 131072
TOKENS = 65536
NEXT = 65536
N_DEV = 128


def draw_hot_slots(key, part):
    key_list = jax.random.split(jax.random.fold_in(key, 11), N_DEV * N_DEV)
    chosen = jax.vmap(lambda single: jax.random.permutation(single, HOT_DEV)[:HB])(key_list)
    owner_of = (jnp.arange(N_DEV * N_DEV) % N_DEV)[:, None]
    return (owner_of * HOT_DEV + chosen).reshape(-1).astype(jnp.int32)


def draw_evict_dest(key, part):
    first, second, third, fourth = jax.random.split(jax.random.fold_in(key, 23), 4)
    owner_heat = jax.random.randint(first, (N_DEV, 1), 0, 3)
    filled = jnp.minimum(EVB, jax.random.randint(second, (N_DEV, N_DEV), 0, EVB + 1) + owner_heat)
    corner = jax.random.randint(fourth, (2,), 0, N_DEV)
    filled = filled.at[corner[0], corner[1]].set(EVB)
    is_live = jnp.arange(EVB)[None, None, :] < filled[:, :, None]
    row_pick = jax.random.randint(third, (N_DEV, N_DEV, EVB), 0, OWN_DEV)
    return jnp.where(is_live, row_pick, -1).astype(jnp.int32)


def plant(result, own_key, least, largest):
    extent = result.shape
    place = [jax.random.randint(jax.random.fold_in(own_key, axis), (), 0, extent[axis]) for axis in range(len(extent))]
    result = result.at[tuple(place)].set(least)
    longest = extent.index(max(extent))
    place[longest] = (place[longest] + 1) % extent[longest]
    return result.at[tuple(place)].set(largest)


def with_spikes(values, own_key, source, target, shards_of, factor):
    def block_of(dim):
        return (jnp.arange(values.shape[dim]) // (values.shape[dim] // shards_of)).reshape((-1,) + (1,) * (values.ndim - 1 - dim))

    near = jax.random.permutation(own_key, shards_of)[block_of(target)]
    other_side = (block_of(target) + shards_of // 2) % shards_of
    return jnp.where((block_of(source) == near) | (block_of(source) == other_side), factor * values, values)


def level_of(rng, extent, pieces, low, largest):
    gain, own = 1.0, jax.random.fold_in(rng, 6)
    for axis_at, blocks in pieces:
        draws = jnp.exp(jax.random.uniform(jax.random.fold_in(own, axis_at), (blocks,), jnp.float32, low / len(pieces), largest / len(pieces)))
        gain = gain * jnp.repeat(draws, extent[axis_at] // blocks).reshape([-1 if axis == axis_at else 1 for axis in range(len(extent))])
    return gain


def centred(own_key, shape, scale, most, pieces=(), kind=jnp.bfloat16):
    array = scale * jax.random.normal(own_key, shape, jnp.float32)
    if pieces:
        array = array * level_of(own_key, shape, pieces, -0.22, 0.18)
    return jnp.clip(array, -most, most).astype(kind)


def heavy_noise(stream_key, extent, scale, bound, pieces, heavy, dtype=jnp.bfloat16):
    result = scale * jax.random.normal(stream_key, extent, jnp.float32)
    if pieces:
        result = result * level_of(stream_key, extent, pieces, -0.22, 0.18)
    return jnp.clip(with_spikes(result, jax.random.fold_in(stream_key, 3), *heavy), -bound, bound).astype(dtype)


def setup_inputs(seed: int = 0) -> dict:
    splits = jax.random.split(jax.random.key(seed), 15)
    return {
        "upstream": heavy_noise(splits[0], (TOKENS, D), 1.0, 24.0, ((0, 128),), (0, 1, 128, 5.5)),
        "bag": plant(jax.random.randint(splits[1], (TOKENS, F), 0, (HB + EVB) * N_DEV), jax.random.fold_in(splits[1], 1), 0, ((HB + EVB) * N_DEV) - 1).astype(jnp.int32),
        "next_bag": plant(jax.random.randint(splits[2], (NEXT, F), 0, HB * N_DEV), jax.random.fold_in(splits[2], 1), 0, (HB * N_DEV) - 1).astype(jnp.int32),
        "hot_slots": draw_hot_slots(jax.random.fold_in(splits[14], 71), 0),
        "evict_dest": draw_evict_dest(jax.random.fold_in(splits[14], 71), 0),
        "hot_cache": centred(splits[5], (N_DEV * HOTC, E), 1.0, 6.0, ((0, 128),), jnp.float32),
        "evict_cache": centred(splits[6], (N_DEV * EVC, E), 1.0, 6.0, ((0, 128),), jnp.float32),
        "hot_table": centred(splits[7], (HOT, E), 1.0, 6.0, ((0, 128),), jnp.float32),
        "hot_accum": jnp.clip(jnp.exp(math.log(100.0) - 4.6051702 * jax.random.uniform(splits[8], (HOT, E), jnp.float32) ** level_of(splits[8], (HOT, E), ((0, 128),), -0.2, 0.2)), 1.0, 100.0),
        "owner_table": centred(splits[9], (OWNED, E), 1.0, 6.0, ((0, 128),), jnp.float32),
        "owner_accum": jnp.clip(jnp.exp(math.log(30.0) - 3.4011974 * jax.random.uniform(splits[10], (OWNED, E), jnp.float32) ** level_of(splits[10], (OWNED, E), ((0, 128),), -0.2, 0.2)), 1.0, 30.0),
        "cross_w": centred(splits[11], (2, D, D), D ** -0.5, 0.1875, ((2, 128),), jnp.float32),
        "cross_b": centred(splits[12], (2, D), 0.5, 3.0, ((1, 128),), jnp.float32),
        "cross_accum": jnp.clip(jnp.exp(math.log(1000000) - 4.6051702 * jax.random.uniform(splits[13], (2, D, D), jnp.float32) ** level_of(splits[13], (2, D, D), ((2, 128),), -0.2, 0.2)), 10000.0, 1000000),
    }


row_rate = 0.05
weight_rate = 0.005
bias_rate = 0.0002
epsilon = 1e-10

def adagrad(params, accumulator, gradient, step_rate):
    updated = accumulator + gradient * gradient
    return (params - step_rate * gradient / (jnp.sqrt(updated) + epsilon), updated)

def rounded(values):
    return lax.optimization_barrier(values.astype(jnp.bfloat16)).astype(jnp.float32)

def device_pass(weights, biases, grad_in, bag_rows, slot_values):
    samples = bag_rows.shape[0]
    features = jnp.take(slot_values, bag_rows.reshape(-1), axis=0).reshape(samples, -1)
    feat_bf = features.astype(jnp.bfloat16)
    proj_one = jnp.dot(feat_bf, weights[0], preferred_element_type=jnp.float32) + biases[0]
    layer_one = features * proj_one + features
    layer_bf = layer_one.astype(jnp.bfloat16)
    proj_two = jnp.dot(layer_bf, weights[1], preferred_element_type=jnp.float32) + biases[1]
    grad_out = grad_in.astype(jnp.float32)
    grad_two = grad_out * features
    grad_two_bf = grad_two.astype(jnp.bfloat16)
    weight_two = jnp.dot(layer_bf.T, grad_two_bf, preferred_element_type=jnp.float32)
    bias_two = lax.optimization_barrier(jnp.sum(grad_two, axis=0))
    grad_layer = grad_out + jnp.dot(grad_two_bf, weights[1].T, preferred_element_type=jnp.float32)
    grad_one = grad_layer * features
    grad_one_bf = grad_one.astype(jnp.bfloat16)
    weight_one = jnp.dot(feat_bf.T, grad_one_bf, preferred_element_type=jnp.float32)
    bias_one = lax.optimization_barrier(jnp.sum(grad_one, axis=0))
    grad_feat = grad_out * proj_two + grad_layer * (proj_one + 1.0)
    grad_feat = grad_feat + jnp.dot(grad_one_bf, weights[0].T, preferred_element_type=jnp.float32)
    flat_grad = rounded(grad_feat).reshape(-1, slot_values.shape[1])
    slot_grad = jax.ops.segment_sum(flat_grad, bag_rows.reshape(-1), num_segments=slot_values.shape[0])
    return (weight_one, weight_two, bias_one, bias_two, slot_grad)

def reference(upstream, bag, next_bag, hot_slots, evict_dest, hot_cache, evict_cache, hot_table, hot_accum, owner_table, owner_accum, cross_w, cross_b, cross_accum):
    weights = cross_w.astype(jnp.bfloat16)
    biases = rounded(cross_b)
    hot_count = HB * N_DEV
    evict_count = EVB * N_DEV
    inputs = (upstream.reshape(N_DEV, TOK_DEV, D), bag.reshape(N_DEV, TOK_DEV, F), hot_cache.reshape(N_DEV, hot_count, E), evict_cache.reshape(N_DEV, evict_count, E), hot_slots.reshape(N_DEV, hot_count))

    def visit(carry, item):
        weight_sum, bias_sum, hot_grad = carry
        grad_in, bag_rows, hot_rows, evict_rows, hot_ids = item
        slot_values = jnp.concatenate([hot_rows, evict_rows], axis=0)
        weight_one, weight_two, bias_one, bias_two, slot_grad = device_pass(weights, biases, grad_in, bag_rows, slot_values)
        weight_sum = weight_sum + jnp.stack([weight_one, weight_two])
        bias_sum = bias_sum + jnp.stack([bias_one, bias_two])
        hot_grad = hot_grad.at[hot_ids].add(slot_grad[:hot_count])
        return ((weight_sum, bias_sum, hot_grad), slot_grad[hot_count:])
    start = (jnp.zeros((2, D, D), jnp.float32), jnp.zeros((2, D), jnp.float32), jnp.zeros((HOT_DEV * N_DEV, E), jnp.float32))
    (weight_sum, bias_sum, hot_grad), evicted = lax.scan(visit, start, inputs)
    hot_new, hot_accum_new = adagrad(hot_table, hot_accum, hot_grad, row_rate)
    moved = evicted.reshape(N_DEV, N_DEV, EVB, E).transpose(1, 0, 2, 3)
    owner_base = (jnp.arange(N_DEV).astype(jnp.int32) * OWN_DEV)[:, None, None]
    targets = jnp.where(evict_dest >= 0, owner_base + evict_dest, N_DEV * OWN_DEV).astype(jnp.int32)
    owner_grad = jax.ops.segment_sum(moved.reshape(-1, E), targets.reshape(-1), num_segments=N_DEV * OWN_DEV + 1)[:N_DEV * OWN_DEV]
    owner_new, owner_accum_new = adagrad(owner_table, owner_accum, owner_grad, row_rate)
    cross_w_new, unused = adagrad(cross_w, cross_accum, weight_sum, weight_rate)
    cross_b_new = cross_b - bias_rate * bias_sum
    held_rows = hot_new[hot_slots]
    slot_base = (jnp.arange(N_DEV).astype(jnp.int32) * hot_count)[:, None, None]
    picks = (slot_base + next_bag.reshape(N_DEV, NEXT_DEV, F)).astype(jnp.int32)
    next_feat = held_rows[picks.reshape(-1)].reshape(N_DEV * NEXT_DEV, D)
    proj = jnp.dot(next_feat.astype(jnp.bfloat16), cross_w_new[0].astype(jnp.bfloat16), preferred_element_type=jnp.float32) + rounded(cross_b_new[0])
    next_first = (next_feat * proj + next_feat).astype(jnp.bfloat16)
    return (next_first, hot_new, hot_accum_new, owner_new, owner_accum_new, cross_w_new, cross_b_new)
```

```python
import functools

import jax
import jax.numpy as jnp
from jax import lax
from jax.experimental import pallas as pl
from jax.experimental.pallas import tpu as pltpu
from jax.sharding import PartitionSpec as P

row_rate = 0.05
weight_rate = 0.005
bias_rate = 0.0002
epsilon = 1e-10

MESH = pl.DeviceIdType.MESH
F32 = jnp.float32
BF16 = jnp.bfloat16
HIGH = lax.Precision.HIGHEST
STRIDE = (32, 8, 2)
TILES = ((0, 1, 2, 6), (3, 4, 5, 7))
GATHER = ((0, 3, (2, 1, 0)), (3, 3, (1, 0, 2)), (6, 3, (0, 2, 1)))
GATHER_NEXT = ((0, 2, (2, 1, 0)), (2, 2, (1, 0, 2)), (4, 1, (0, 2, 1)))


def place():
    me = lax.axis_index("dev")
    core = lax.rem(me, 2)
    chip = me // 2
    coords = (chip // 16, lax.rem(chip // 4, 4), lax.rem(chip, 4))
    return me, core, coords


def step_to(me, coords, axis, by):
    at = coords[axis]
    return me + (lax.rem(at + by + 4, 4) - at) * STRIDE[axis]


def sibling_of(me, core):
    return me + 1 - 2 * core


def remote(source, target, send, recv, device):
    return pltpu.make_async_remote_copy(
        src_ref=source, dst_ref=target, send_sem=send, recv_sem=recv, device_id=(device,), device_id_type=MESH
    )


def greet(me, core, coords):
    barrier = pltpu.get_barrier_semaphore()
    for axis in range(3):
        for by in (1, -1):
            pl.semaphore_signal(barrier, inc=1, device_id=(step_to(me, coords, axis, by),), device_id_type=MESH)
    pl.semaphore_signal(barrier, inc=1, device_id=(sibling_of(me, core),), device_id_type=MESH)
    pl.semaphore_wait(barrier, 7)


def gather_all(buf, parts, me, core, coords, ring_send, ring_recv, pair_send, pair_recv):
    sends, pairs = [], []

    def view(part, index):
        first, count, _ = part
        return buf.at[(core, pl.ds(first, count), *index)]

    for k in range(3):
        firsts = []
        for p, part in enumerate(parts):
            axis, full = part[2][k], part[2][:k]

            def block(j, half=None, axis=axis, full=full):
                index = list(coords)
                for f in full:
                    index[f] = pl.ds(0, 4)
                if half is not None and full:
                    index[full[0]] = pl.ds(2 * half, 2)
                index[axis] = lax.rem(coords[axis] + j + 4, 4)
                return tuple(index)

            right, left = step_to(me, coords, axis, 1), step_to(me, coords, axis, -1)
            own = view(part, block(0))
            a = remote(own, own, ring_send.at[p, k, 0], ring_recv.at[p, k, 0], right)
            b = remote(own, own, ring_send.at[p, k, 1], ring_recv.at[p, k, 1], left)
            a.start()
            b.start()
            sends += [a, b]

            def pass_on(which, index, p=p, part=part):
                ref = view(part, index)
                copy = remote(ref, ref, pair_send.at[p, which], pair_recv.at[p, which], sibling_of(me, core))
                copy.start()
                pairs.append(copy)

            if k == 2:
                pass_on(0, block(0))
            firsts.append((p, part, a, b, block, right, left, pass_on))
        yield
        seconds = []
        for p, part, a, b, block, right, left, pass_on in firsts:
            a.wait_recv()
            ref = view(part, block(-1, 0))
            c = remote(ref, ref, ring_send.at[p, k, 2], ring_recv.at[p, k, 2], right)
            c.start()
            sends.append(c)
            b.wait_recv()
            d = None
            if k > 0:
                ref = view(part, block(1, 1))
                d = remote(ref, ref, ring_send.at[p, k, 3], ring_recv.at[p, k, 3], left)
                d.start()
                sends.append(d)
            if k == 2:
                pass_on(1, block(-1))
                pass_on(2, block(1))
            seconds.append((c, d, block, pass_on))
        yield
        for c, d, block, pass_on in seconds:
            c.wait_recv()
            if k == 2:
                pass_on(3, block(2, 0))
            if d is not None:
                d.wait_recv()
                if k == 2:
                    pass_on(4, block(2, 1))
    yield
    for copy in pairs:
        copy.wait_recv()
    for copy in sends + pairs:
        copy.wait_send()


def rows(value):
    return value.reshape(-1, value.shape[-1])


def front(
    w_ref, a_ref, b_ref, bag_ref, bag_t_ref, up_ref, hot_ref, evict_ref,
    wg_ref, hot_grad_ref, evict_grad_ref, pair_out,
    own, pair, buf, feat, feat_bf, proj, layer_bf, grad_two, grad_one, rest, grad_feat, values, bias_sum,
    ring_send, ring_recv, pair_send, pair_recv, swap_send, swap_recv,
):
    me, core, coords = place()
    for half in range(2):
        for layer in range(2):
            for j, t in enumerate(TILES[layer]):
                lanes = pl.ds(half * 512 + j * 128, 128)
                own[half, t] = w_ref[layer, :, lanes]
                own[half, 9 + t] = a_ref[layer, :, lanes]
        own[half, 8] = b_ref[...]
    greet(me, core, coords)
    mine = pl.ds(pl.multiple_of(core * 8, 8), 8)
    swap = remote(own.at[1 - core], pair.at[:, mine, :], swap_send, swap_recv, sibling_of(me, core))
    swap.start()
    pair[:, mine, :] = own[core]

    table = jnp.concatenate([hot_ref[...], evict_ref[...]], axis=0)
    high = table.astype(BF16)
    values[:, 0:128] = high
    values[:, 128:256] = (table - high.astype(F32)).astype(BF16)

    swap.wait_recv()
    buf[(core, slice(None), *coords)] = pair[0:9].astype(BF16)
    pair_out[...] = pair[...]

    def look_up(field):
        ids = bag_ref[:, field : field + 1]
        slots = lax.broadcasted_iota(jnp.int32, (ids.shape[0], 768), 1)
        pick = jnp.where(slots == ids, 1.0, 0.0).astype(BF16)
        found = jnp.dot(pick, values[...], preferred_element_type=F32)
        lanes = pl.ds(field * 128, 128)
        feat_bf[:, lanes] = found[:, 0:128].astype(BF16)
        value = found[:, 0:128] + found[:, 128:256]
        feat[:, lanes] = value
        two = up_ref[:, lanes].astype(F32) * value
        grad_two[:, lanes] = two.astype(BF16)
        bias_sum[1:2, lanes] = jnp.sum(two, axis=0, keepdims=True)

    bias_sum[...] = jnp.zeros_like(bias_sum)
    field = 0
    for _ in gather_all(buf, GATHER, me, core, coords, ring_send, ring_recv, pair_send, pair_recv):
        for _ in range(2):
            if field < 8:
                look_up(field)
                field += 1
    while field < 8:
        look_up(field)
        field += 1
    swap.wait_send()

    def by_rows(layer, block):
        return jnp.concatenate([rows(buf[h, t, block]) for h in range(2) for t in TILES[layer]], axis=1)

    def by_columns(layer, block):
        picked = TILES[layer][2 * (block % 2) : 2 * (block % 2) + 2]
        return jnp.concatenate([rows(buf[block // 2, t]) for t in picked], axis=1)

    def turned(a, b):
        return lax.dot_general(a, b, (((1,), (1,)), ((), ())), preferred_element_type=F32)

    def outer(a, b):
        return lax.dot_general(a, b, (((0,), (0,)), ((), ())), preferred_element_type=F32)

    def bias_of(layer, block):
        lane = lax.broadcasted_iota(jnp.int32, (8, 128), 1)
        pick = jnp.where(lane == layer, 1.0, 0.0).astype(BF16)
        return turned(pick, rows(buf[0, 8, block]))[0:1]

    def put(layer, block, value):
        value = value.astype(BF16)
        for h in range(2):
            for j, t in enumerate(TILES[layer]):
                at = h * 512 + j * 128
                wg_ref[h, t, block] = value[:, at : at + 128].reshape(4, 4, 16, 128)

    for n in range(4):
        lanes = pl.ds(n * 256, 256)
        one = turned(feat_bf[...], by_rows(0, n)) + bias_of(0, n)
        proj[:, lanes] = one
        value = feat[:, lanes]
        layer_bf[:, lanes] = (value * one + value).astype(BF16)
    for n in range(4):
        lanes = pl.ds(n * 256, 256)
        put(1, n, outer(grad_two[:, lanes], layer_bf[...]))
    for n in range(4):
        lanes = pl.ds(n * 256, 256)
        up = up_ref[:, lanes].astype(F32)
        back = up + jnp.dot(grad_two[...], by_columns(1, n), preferred_element_type=F32)
        one = back * feat[:, lanes]
        grad_one[:, lanes] = one.astype(BF16)
        bias_sum[0:1, lanes] = jnp.sum(one, axis=0, keepdims=True)
        two = turned(layer_bf[...], by_rows(1, n)) + bias_of(1, n)
        rest[:, lanes] = up * two + back * (proj[:, lanes] + 1.0)
    turned_sum = bias_sum[...].T.astype(BF16).reshape(4, 4, 4, 16, 128)
    wg_ref[0, 8] = turned_sum
    wg_ref[1, 8] = turned_sum
    for n in range(4):
        lanes = pl.ds(n * 256, 256)
        put(0, n, outer(grad_one[:, lanes], feat_bf[...]))
    for n in range(4):
        lanes = pl.ds(n * 256, 256)
        last = jnp.dot(grad_one[...], by_columns(0, n), preferred_element_type=F32)
        grad_feat[:, lanes] = (rest[:, lanes] + last).astype(BF16)
    total = jnp.zeros((768, 128), F32)
    for f in range(8):
        ids = bag_t_ref[f : f + 1, :]
        slots = lax.broadcasted_iota(jnp.int32, (768, ids.shape[1]), 0)
        pick = jnp.where(slots == ids, 1.0, 0.0).astype(BF16)
        total += jnp.dot(pick, grad_feat[:, f * 128 : f * 128 + 128], preferred_element_type=F32)
    hot_grad_ref[...] = total[0:512]
    evict_grad_ref[...] = total[512:768]


def middle(
    wg_ref, pair_ref, next_ref, w_new_ref, b_new_ref,
    sib, sums, got1, acc2, send2, got2, acc3, got3, total, buf, fresh, other,
    rs_send, rs_recv, sib_send, sib_recv, ring_send, ring_recv, pair_send, pair_recv, swap_send, swap_recv,
):
    me, core, coords = place()
    greet(me, core, coords)
    near = sibling_of(me, core)
    swaps, sends = [], []
    for p in range(3):
        tiles = pl.ds(3 * p, 3)
        copy = remote(wg_ref.at[1 - core, tiles], sib.at[tiles], sib_send.at[p], sib_recv.at[p], near)
        copy.start()
        swaps.append(copy)

    orders = [part[2][::-1] for part in GATHER]

    def launch(source, target, p, k, i, device):
        copy = remote(source, target, rs_send.at[p, k, i], rs_recv.at[p, k, i], device)
        copy.start()
        sends.append(copy)
        return copy

    def ends(p, k):
        axis = orders[p][k]
        return step_to(me, coords, axis, 1), step_to(me, coords, axis, -1)

    def pick(p, k, j, half=None):
        order = orders[p]
        axes = sorted(order[k:])
        index = []
        for axis in axes:
            if axis == order[k]:
                index.append(lax.rem(coords[axis] + j + 4, 4))
            elif half is not None and axis == order[2]:
                index.append(pl.ds(2 * half, 2))
            else:
                index.append(pl.ds(0, 4))
        return tuple(index)

    def inner(p, k, half):
        order = orders[p]
        axes = [axis for axis in sorted(order[k:]) if axis != order[k]]
        return tuple(pl.ds(2 * half, 2) if half is not None and axis == order[2] else pl.ds(0, 4) for axis in axes)

    def widen(value):
        return value.astype(F32)

    flights = []
    for p in range(3):
        tiles = pl.ds(3 * p, 3)
        swaps[p].wait_recv()
        for y in range(4):
            sums[tiles, y] = (widen(wg_ref[core, tiles, y]) + widen(sib[tiles, y])).astype(BF16)
        right, left = ends(p, 0)
        flights.append((
            launch(sums.at[(tiles, *pick(p, 0, 2, 0))], got1.at[(p, 0, slice(None), *inner(p, 0, 0))], p, 0, 0, right),
            launch(sums.at[(tiles, *pick(p, 0, 1, 1))], got1.at[(p, 1, slice(None), *inner(p, 0, 1))], p, 0, 1, right),
            launch(sums.at[(tiles, *pick(p, 0, 2, 1))], got1.at[(p, 0, slice(None), *inner(p, 0, 1))], p, 0, 2, left),
            launch(sums.at[(tiles, *pick(p, 0, -1, 0))], got1.at[(p, 2, slice(None), *inner(p, 0, 0))], p, 0, 3, left),
        ))
    later = []
    for p in range(3):
        tiles = pl.ds(3 * p, 3)
        right, left = ends(p, 0)
        first, _, third, _ = flights[p]
        pair_of = []
        for copy, j, half, slot, i, device in ((first, 1, 0, 1, 4, right), (third, -1, 1, 2, 5, left)):
            copy.wait_recv()
            at = (tiles, *pick(p, 0, j, half))
            there = (slice(None), *inner(p, 0, half))
            sums[at] = (widen(wg_ref[(core, *at)]) + widen(sib[at]) + widen(got1[(p, 0, *there)])).astype(BF16)
            pair_of.append(launch(sums.at[at], got1.at[(p, slot, *there)], p, 0, i, device))
        later.append(pair_of)
    for p in range(3):
        tiles = pl.ds(3 * p, 3)
        for copy in (flights[p][1], flights[p][3], *later[p]):
            copy.wait_recv()
        at = (tiles, *pick(p, 0, 0))
        acc2[p] = widen(wg_ref[(core, *at)]) + widen(sib[at]) + widen(got1[p, 1]) + widen(got1[p, 2])
        send2[p] = acc2[p].astype(BF16)
        right, left = ends(p, 1)
        flights[p] = (
            launch(send2.at[(p, slice(None), *pick(p, 1, 2, 0))], got2.at[(p, 0, slice(None), *inner(p, 1, 0))], p, 1, 0, right),
            launch(send2.at[(p, slice(None), *pick(p, 1, 1, 1))], got2.at[(p, 1, slice(None), *inner(p, 1, 1))], p, 1, 1, right),
            launch(send2.at[(p, slice(None), *pick(p, 1, 2, 1))], got2.at[(p, 0, slice(None), *inner(p, 1, 1))], p, 1, 2, left),
            launch(send2.at[(p, slice(None), *pick(p, 1, -1, 0))], got2.at[(p, 2, slice(None), *inner(p, 1, 0))], p, 1, 3, left),
        )
    for p in range(3):
        right, left = ends(p, 1)
        first, _, third, _ = flights[p]
        pair_of = []
        for copy, j, half, slot, i, device in ((first, 1, 0, 1, 4, right), (third, -1, 1, 2, 5, left)):
            copy.wait_recv()
            at = (p, slice(None), *pick(p, 1, j, half))
            there = (slice(None), *inner(p, 1, half))
            send2[at] = (acc2[at] + widen(got2[(p, 0, *there)])).astype(BF16)
            pair_of.append(launch(send2.at[at], got2.at[(p, slot, *there)], p, 1, i, device))
        later[p] = pair_of
    for p in range(3):
        for copy in (flights[p][1], flights[p][3], *later[p]):
            copy.wait_recv()
        acc3[p] = acc2[(p, slice(None), *pick(p, 1, 0))] + widen(got2[p, 1]) + widen(got2[p, 2])
        right, left = ends(p, 2)
        flights[p] = (
            launch(acc3.at[(p, slice(None), *pick(p, 2, 2))], got3.at[p, 0], p, 2, 0, right),
            launch(acc3.at[(p, slice(None), *pick(p, 2, -1))], got3.at[p, 2], p, 2, 3, left),
        )
    for p in range(3):
        right, left = ends(p, 2)
        flights[p][0].wait_recv()
        at = (p, slice(None), *pick(p, 2, 1))
        acc3[at] = acc3[at] + got3[p, 0]
        later[p] = launch(acc3.at[at], got3.at[p, 1], p, 2, 4, right)
    for p in range(3):
        flights[p][1].wait_recv()
        later[p].wait_recv()
        total[pl.ds(3 * p, 3)] = acc3[(p, slice(None), *pick(p, 2, 0))] + got3[p, 1] + got3[p, 2]

    grad = total[0:8]
    fresh[...] = pair_ref[0:8] - weight_rate * grad / (jnp.sqrt(pair_ref[9:17] + grad * grad) + epsilon)
    bias = pair_ref[8] - bias_rate * total[8]
    for j, t in enumerate(TILES[0]):
        buf[(core, j, *coords)] = fresh[t].astype(BF16)
    buf[(core, 4, *coords)] = bias.astype(BF16)
    mine = pl.ds(pl.multiple_of(core * 8, 8), 8)
    yours = pl.ds(pl.multiple_of(8 - core * 8, 8), 8)
    total[8] = bias
    b_new_ref[...] = total[8, mine, :]
    swap = remote(fresh.at[:, yours, :], other, swap_send, swap_recv, near)
    swap.start()
    for _ in gather_all(buf, GATHER_NEXT, me, core, coords, ring_send, ring_recv, pair_send, pair_recv):
        pass
    swap.wait()
    for layer in range(2):
        for h in range(2):
            for j, t in enumerate(TILES[layer]):
                at = h * 512 + j * 128
                w_new_ref[layer, :, at : at + 128] = jnp.where(core == h, fresh[t, mine, :], other[t])
    for h in range(2):
        for t in range(5):
            next_ref[h, t] = buf[h, t]
    for copy in swaps + sends:
        copy.wait_send()


def shared(ids_ref, arrived_ref, table_ref, accum_ref, new_ref, accum_new_ref, back_ref):
    wanted = lax.broadcasted_iota(jnp.int32, (512, 64), 1)
    pick = jnp.where(wanted == ids_ref[...], 1.0, 0.0)
    grad = lax.dot_general(pick, arrived_ref[...], (((0,), (0,)), ((), ())), precision=HIGH, preferred_element_type=F32)
    updated = accum_ref[...] + grad * grad
    new = table_ref[...] - row_rate * grad / (jnp.sqrt(updated) + epsilon)
    new_ref[...] = new
    accum_new_ref[...] = updated
    back_ref[...] = jnp.dot(pick, new, precision=HIGH, preferred_element_type=F32)


def owned(ids_ref, moved_ref, table_ref, accum_ref, new_ref, accum_new_ref):
    moved = moved_ref[...]
    for n in range(4):
        at = pl.ds(n * 256, 256)
        wanted = lax.broadcasted_iota(jnp.int32, (256, 256), 0) + n * 256
        pick = jnp.where(wanted == ids_ref[...], 1.0, 0.0)
        grad = jnp.dot(pick, moved, precision=HIGH, preferred_element_type=F32)
        updated = accum_ref[at, :] + grad * grad
        new_ref[at, :] = table_ref[at, :] - row_rate * grad / (jnp.sqrt(updated) + epsilon)
        accum_new_ref[at, :] = updated


def ahead(bag_ref, held_ref, next_ref, out_ref, values, feat, feat_bf):
    held = held_ref[...]
    high = held.astype(BF16)
    values[:, 0:128] = high
    values[:, 128:256] = (held - high.astype(F32)).astype(BF16)
    for f in range(8):
        ids = bag_ref[:, f : f + 1]
        slots = lax.broadcasted_iota(jnp.int32, (ids.shape[0], 512), 1)
        pick = jnp.where(slots == ids, 1.0, 0.0).astype(BF16)
        found = jnp.dot(pick, values[...], preferred_element_type=F32)
        lanes = pl.ds(f * 128, 128)
        feat_bf[:, lanes] = found[:, 0:128].astype(BF16)
        feat[:, lanes] = found[:, 0:128] + found[:, 128:256]
    nt = (((1,), (1,)), ((), ()))
    for n in range(4):
        lanes = pl.ds(n * 256, 256)
        weight = jnp.concatenate([rows(next_ref[h, t, n]) for h in range(2) for t in range(4)], axis=1)
        proj = lax.dot_general(feat_bf[...], weight, nt, preferred_element_type=F32)
        lane = lax.broadcasted_iota(jnp.int32, (8, 128), 1)
        pick = jnp.where(lane == 0, 1.0, 0.0).astype(BF16)
        proj = proj + lax.dot_general(pick, rows(next_ref[0, 4, n]), nt, preferred_element_type=F32)[0:1]
        value = feat[:, lanes]
        out_ref[:, lanes] = (value * proj + value).astype(BF16)


VM = pl.BlockSpec(memory_space=pltpu.VMEM)
DMA = pltpu.SemaphoreType.DMA
LIMIT = 60 * 1024 * 1024


def call(body, ins, outs, scratch, cost, collective=None):
    if collective is None:
        params = pltpu.CompilerParams(vmem_limit_bytes=LIMIT)
    else:
        params = pltpu.CompilerParams(vmem_limit_bytes=LIMIT, collective_id=collective, has_side_effects=True)
    return pl.pallas_call(
        body,
        out_shape=tuple(jax.ShapeDtypeStruct(s, d) for s, d in outs),
        in_specs=[VM] * ins,
        out_specs=tuple(VM for _ in outs),
        scratch_shapes=scratch,
        compiler_params=params,
        cost_estimate=pl.CostEstimate(flops=cost, bytes_accessed=8_000_000, transcendentals=0),
    )


def local(
    upstream, bag, next_bag, hot_slots, evict_dest, hot_cache, evict_cache, hot_table, hot_accum, owner_table, owner_accum,
    cross_w, cross_b, cross_accum,
):
    me = lax.axis_index("dev")
    biases = jnp.pad(cross_b.T, ((0, 0), (0, 126)))
    ids = hot_slots.reshape(128, 1, 4)
    arrived_ids = lax.all_to_all(ids, "dev", split_axis=0, concat_axis=0, tiled=True)
    local_ids = (arrived_ids - me * 64).reshape(512, 1)

    ring = [DMA((3, 3, 4)), DMA((3, 3, 4)), DMA((3, 5)), DMA((3, 5)), DMA, DMA]
    wide = (512, 1024)
    wg, hot_grad, evict_grad, pair = call(
        front, 8,
        [((2, 9, 4, 4, 4, 16, 128), BF16), ((512, 128), F32), ((256, 128), F32), ((17, 16, 128), F32)],
        [
            pltpu.VMEM((2, 17, 8, 128), F32), pltpu.VMEM((17, 16, 128), F32), pltpu.VMEM((2, 9, 4, 4, 4, 16, 128), BF16),
            pltpu.VMEM(wide, F32), pltpu.VMEM(wide, BF16), pltpu.VMEM(wide, F32), pltpu.VMEM(wide, BF16),
            pltpu.VMEM(wide, BF16), pltpu.VMEM(wide, BF16), pltpu.VMEM(wide, F32),
            pltpu.VMEM(wide, BF16), pltpu.VMEM((768, 256), BF16), pltpu.VMEM((128, 1024), F32), *ring,
        ],
        8_000_000_000, 1,
    )(
        jnp.swapaxes(cross_w, 1, 2), jnp.swapaxes(cross_accum, 1, 2), biases, bag, bag.T, upstream, hot_cache, evict_cache,
    )
    packed = jnp.concatenate([hot_grad.reshape(128, 4, 128), evict_grad.reshape(128, 2, 128)], axis=1)
    unpacked = lax.all_to_all(packed, "dev", split_axis=0, concat_axis=0, tiled=True)

    block = (4, 4, 16, 128)
    next_w, w_new, b_new = call(
        middle, 2,
        [((2, 5, 4, 4, 4, 16, 128), BF16), ((2, 8, 1024), F32), ((8, 128), F32)],
        [
            pltpu.VMEM((9, 4, 4, 4, 16, 128), BF16), pltpu.VMEM((9, 4, 4, 4, 16, 128), BF16),
            pltpu.VMEM((3, 3, 3, *block), BF16), pltpu.VMEM((3, 3, *block), F32), pltpu.VMEM((3, 3, *block), BF16),
            pltpu.VMEM((3, 3, 3, 4, 16, 128), BF16), pltpu.VMEM((3, 3, 4, 16, 128), F32),
            pltpu.VMEM((3, 3, 3, 16, 128), F32), pltpu.VMEM((9, 16, 128), F32),
            pltpu.VMEM((2, 5, 4, 4, 4, 16, 128), BF16), pltpu.VMEM((8, 16, 128), F32), pltpu.VMEM((8, 8, 128), F32),
            DMA((3, 3, 6)), DMA((3, 3, 6)), DMA((3,)), DMA((3,)), *ring,
        ],
        20_000_000_000, 2,
    )(wg, pair)

    hot_new, hot_accum_new, returned = call(
        shared, 4, [((64, 128), F32), ((64, 128), F32), ((512, 128), F32)], [], 100_000_000,
    )(local_ids, unpacked[:, :4].reshape(512, 128), hot_table, hot_accum)
    held = lax.all_to_all(returned.reshape(128, 4, 128), "dev", split_axis=0, concat_axis=0, tiled=True).reshape(512, 128)
    owner_new, owner_accum_new = call(
        owned, 4, [((1024, 128), F32), ((1024, 128), F32)], [], 1_000_000_000,
    )(evict_dest.reshape(1, 256), unpacked[:, 4:].reshape(256, 128), owner_table, owner_accum)
    (next_first,) = call(
        ahead, 3, [((512, 1024), BF16)],
        [pltpu.VMEM((512, 256), BF16), pltpu.VMEM(wide, F32), pltpu.VMEM(wide, BF16)], 3_000_000_000,
    )(next_bag, held, next_w)
    return (
        next_first, hot_new, hot_accum_new, owner_new, owner_accum_new,
        jnp.swapaxes(w_new, 1, 2), b_new[:, :2].T,
    )


def solution(mesh):
    row, cube = P("dev", None), P(None, None, "dev")
    return jax.shard_map(
        local,
        mesh=mesh,
        in_specs=(row, row, row, P("dev"), P("dev", None, None), row, row, row, row, row, row, cube, P(None, "dev"), cube),
        out_specs=(row, row, row, row, row, cube, P(None, "dev")),
        check_vma=False,
    )
```

```python
import jax
import jax.numpy as jnp
from jax import lax
from jax.experimental import pallas as pl
from jax.experimental.pallas import tpu as pltpu
from jax.sharding import PartitionSpec as P

row_rate = 0.05
weight_rate = 0.005
bias_rate = 0.0002
epsilon = 1e-10

MESH = pl.DeviceIdType.MESH
F32 = jnp.float32
BF16 = jnp.bfloat16
STRIDE = (32, 8, 2)
TILES = ((0, 1, 2, 6), (3, 4, 5, 7))
GATHER = ((0, 3, (2, 1, 0)), (3, 3, (1, 0, 2)), (6, 3, (0, 2, 1)))
GATHER_NEXT = ((0, 2, (2, 1, 0)), (2, 2, (1, 0, 2)), (4, 1, (0, 2, 1)))


def place():
    me = lax.axis_index("dev")
    core = lax.rem(me, 2)
    chip = me // 2
    coords = (chip // 16, lax.rem(chip // 4, 4), lax.rem(chip, 4))
    return me, core, coords


def step_to(me, coords, axis, by):
    at = coords[axis]
    return me + (lax.rem(at + by + 4, 4) - at) * STRIDE[axis]


def sibling_of(me, core):
    return me + 1 - 2 * core


def remote(source, target, send, recv, device):
    return pltpu.make_async_remote_copy(
        src_ref=source, dst_ref=target, send_sem=send, recv_sem=recv, device_id=(device,), device_id_type=MESH
    )


def greet(me, core):
    barrier = pltpu.get_barrier_semaphore()
    pl.semaphore_signal(barrier, inc=1, device_id=(sibling_of(me, core),), device_id_type=MESH)

    def one(i, carry):
        peer = lax.rem(me // 2 + i, 64)
        pl.semaphore_signal(barrier, inc=1, device_id=(peer * 2 + core,), device_id_type=MESH)
        return carry

    lax.fori_loop(1, 64, one, 0)


def all_here():
    pl.semaphore_wait(pltpu.get_barrier_semaphore(), 64)


LINES = (0, -1, 1, 2)
GOES_ON = (1, 1, -1, -1)


def gather_all(buf, parts, me, core, coords, ring_send, ring_recv, pair_send, pair_recv):
    sends, pairs, count = [], [], len(parts)
    near = sibling_of(me, core)

    def move(p, index, i, device):
        first, tiles, _ = parts[p]
        ref = buf.at[(core, pl.ds(first, tiles), *index)]
        copy = remote(ref, ref, ring_send.at[p, i], ring_recv.at[p, i], device)
        copy.start()
        sends.append(copy)
        return copy

    def pass_on(p, index, i):
        first, tiles, _ = parts[p]
        ref = buf.at[(core, pl.ds(first, tiles), *index)]
        copy = remote(ref, ref, pair_send.at[p, i], pair_recv.at[p, i], near)
        copy.start()
        pairs.append(copy)

    def index(p, **at):
        order = parts[p][2]
        out = list(coords)
        out[order[0]] = pl.ds(0, 4)
        if at.get("line") is None:
            out[order[1]] = pl.ds(0, 4)
        else:
            out[order[1]] = lax.rem(coords[order[1]] + at["line"] + 4, 4)
        out[order[2]] = lax.rem(coords[order[2]] + at.get("far", 0) + 4, 4)
        return tuple(out)

    def to(p, k, by):
        return step_to(me, coords, parts[p][2][k], by)

    one = [[move(p, coords, i, to(p, 0, by)) for i, by in enumerate((1, -1, 2))] for p in range(count)]
    yield
    two, right, left, passed = [], [], [], []

    def spread(p, i):
        where = index(p, line=LINES[i])
        right[p][i] = move(p, where, 6 + i, to(p, 2, 1))
        left[p][i] = move(p, where, 10 + i, to(p, 2, -1))

    for p in range(count):
        for copy in one[p]:
            copy.wait_recv()
        where = index(p, line=0)
        two.append([move(p, where, 3 + i, to(p, 1, by)) for i, by in enumerate((1, -1, 2))])
        right.append({})
        left.append({})
        passed.append({})
        spread(p, 0)
    yield

    def arrive(p, i):
        right[p][i].wait_recv()
        if GOES_ON[i] == 1:
            passed[p][i] = move(p, index(p, line=LINES[i], far=-1), 14 + i, to(p, 2, 1))
        pass_on(p, index(p, line=LINES[i], far=-1), 1 + i)
        left[p][i].wait_recv()
        if GOES_ON[i] == -1:
            passed[p][i] = move(p, index(p, line=LINES[i], far=1), 14 + i, to(p, 2, -1))
        pass_on(p, index(p, line=LINES[i], far=1), 5 + i)

    for i in (1, 2):
        for p in range(count):
            two[p][i - 1].wait_recv()
            spread(p, i)
    yield
    for p in range(count):
        arrive(p, 0)
    yield
    for p in range(count):
        two[p][2].wait_recv()
        spread(p, 3)
        pass_on(p, index(p), 0)
    yield
    for i in (1, 2, 3):
        for p in range(count):
            arrive(p, i)
        yield
    for i in range(4):
        for p in range(count):
            passed[p][i].wait_recv()
            pass_on(p, index(p, line=LINES[i], far=2), 9 + i)
        yield
    for copy in pairs:
        copy.wait_recv()
    for copy in sends + pairs:
        copy.wait_send()


def rows(value):
    return value.reshape(-1, value.shape[-1])


def turned(a, b):
    return lax.dot_general(a, b, (((1,), (1,)), ((), ())), preferred_element_type=F32)


def outer(a, b):
    return lax.dot_general(a, b, (((0,), (0,)), ((), ())), preferred_element_type=F32)


def iota(shape, dim):
    return lax.broadcasted_iota(jnp.int32, shape, dim)


def as_mask(hit, kind=BF16):
    return jnp.where(hit, 1.0, 0.0).astype(kind)


def halves_of(value):
    high = value.astype(BF16)
    return jnp.concatenate([high, (value - high.astype(F32)).astype(BF16)], axis=1)


def joined(value):
    return value[:, 0:128] + value[:, 128:256]


def widen(value):
    return value.astype(F32)


def step(
    w_ref, a_ref, b_ref, bag_t_ref, next_t_ref, ids_ref, dest_ref, up_ref, hot_ref, evict_ref, table_ref, accum_ref, owner_ref,
    owner_accum_ref,
    out_ref, hot_new_ref, hot_accum_new_ref, owner_new_ref, owner_accum_new_ref, w_new_ref, b_new_ref,
    own, pair, buf, bag, feat, feat_bf, proj, layer_bf, grad_two, grad_one, back, grad_feat, values, bias_sum,
    wg, sib, sums, got1, acc2, send2, got2, acc3, got3, total, fresh, other, buf_next,
    slots, arrived, gathered, split, reply, answer, held,
    ring_send, ring_recv, pair_send, pair_recv, swap_send, swap_recv,
    rs_send, rs_recv, sib_send, sib_recv, ring2_send, ring2_recv, pair2_send, pair2_recv,
    all_send, all_recv, near_send, near_recv,
):
    me, core, coords = place()
    chip = me // 2
    near = sibling_of(me, core)
    mine = pl.ds(pl.multiple_of(core * 8, 8), 8)
    yours = pl.ds(pl.multiple_of(8 - core * 8, 8), 8)

    greet(me, core)
    for half in range(2):
        for layer in range(2):
            for j, t in enumerate(TILES[layer]):
                lanes = pl.ds(half * 512 + j * 128, 128)
                own[half, t] = w_ref[layer, :, lanes]
                own[half, 9 + t] = a_ref[layer, :, lanes]
    bias_tile = jnp.zeros((8, 128), F32)
    for layer in range(2):
        spread = jnp.where(iota((8, 8), 0) == iota((8, 8), 1), jnp.broadcast_to(b_ref[layer : layer + 1, :], (8, 8)), 0.0)
        column = jnp.sum(spread, axis=1, keepdims=True)
        bias_tile = jnp.where(iota((8, 128), 1) == layer, column, bias_tile)
    own[0, 8] = bias_tile
    own[1, 8] = bias_tile
    values[0:512] = halves_of(hot_ref[...])
    values[512:768] = halves_of(evict_ref[...])
    bag[...] = bag_t_ref[...].T
    bias_sum[...] = jnp.zeros_like(bias_sum)
    all_here()
    swap = remote(own.at[1 - core], pair.at[:, mine, :], swap_send.at[0], swap_recv.at[0], near)
    swap.start()
    pair[:, mine, :] = own[core]
    swap.wait_recv()
    buf[(core, slice(None), *coords)] = pair[0:9].astype(BF16)

    def look_up(field):
        ids = bag[:, field : field + 1]
        found = jnp.dot(as_mask(iota((512, 768), 1) == ids), values[...], preferred_element_type=F32)
        lanes = pl.ds(field * 128, 128)
        feat_bf[:, lanes] = found[:, 0:128].astype(BF16)
        value = joined(found)
        feat[:, lanes] = value
        two = widen(up_ref[:, lanes]) * value
        grad_two[:, lanes] = two.astype(BF16)
        bias_sum[1:2, lanes] = jnp.sum(two, axis=0, keepdims=True)

    field = 0
    for _ in gather_all(buf, GATHER, me, core, coords, ring_send, ring_recv, pair_send, pair_recv):
        for _ in range(2):
            if field < 8:
                look_up(field)
                field += 1

    def by_rows(layer, block):
        return jnp.concatenate([rows(buf[h, t, block]) for h in range(2) for t in TILES[layer]], axis=1)

    def by_columns(layer, block):
        picked = TILES[layer][2 * (block % 2) : 2 * (block % 2) + 2]
        return jnp.concatenate([rows(buf[block // 2, t]) for t in picked], axis=1)

    def bias_of(layer, block):
        return turned(as_mask(iota((8, 128), 1) == layer), rows(buf[0, 8, block]))[0:1]

    def put(layer, block, value):
        value = value.astype(BF16)
        for h in range(2):
            for j, t in enumerate(TILES[layer]):
                at = h * 512 + j * 128
                wg[h, t, block] = value[:, at : at + 128].reshape(4, 4, 16, 128)

    orders = [part[2][::-1] for part in GATHER]
    sends, flights, later, thirds = [], {}, {}, {}

    def launch(source, target, p, i, device):
        copy = remote(source, target, rs_send.at[p, i], rs_recv.at[p, i], device)
        copy.start()
        sends.append(copy)
        return copy

    def to(p, k, by):
        return step_to(me, coords, orders[p][k], by)

    def pick(p, k, j, half=None):
        order, index = orders[p], []
        for axis in sorted(order[k:]):
            if axis == order[k]:
                index.append(lax.rem(coords[axis] + j + 4, 4))
            elif half is not None and axis == order[2]:
                index.append(pl.ds(2 * half, 2))
            else:
                index.append(pl.ds(0, 4))
        return tuple(index)

    def inner(p, half):
        order = orders[p]
        return tuple(pl.ds(2 * half, 2) if axis == order[2] else pl.ds(0, 4) for axis in sorted(order[1:]))

    def share(p):
        tiles = pl.ds(3 * p, 3)
        copy = remote(wg.at[1 - core, tiles], sib.at[tiles], sib_send.at[p], sib_recv.at[p], near)
        copy.start()
        sends.append(copy)
        flights[p] = copy

    def reduce_first(p):
        tiles = pl.ds(3 * p, 3)
        flights[p].wait_recv()
        for y in range(4):
            sums[tiles, y] = (widen(wg[core, tiles, y]) + widen(sib[tiles, y])).astype(BF16)

        def block(j, half, slot, i, by):
            at, there = (tiles, *pick(p, 0, j, half)), (slice(None), *inner(p, half))
            return launch(sums.at[at], got1.at[(p, slot, *there)], p, i, to(p, 0, by))

        flights[p] = (block(2, 0, 0, 0, 1), block(2, 1, 0, 2, -1), block(1, 1, 1, 1, 1), block(-1, 0, 2, 3, -1))

    def reduce_on(p):
        tiles = pl.ds(3 * p, 3)
        pair_of = []
        for copy, j, half, slot, i in ((flights[p][0], 1, 0, 1, 4), (flights[p][1], -1, 1, 2, 5)):
            copy.wait_recv()
            at, there = (tiles, *pick(p, 0, j, half)), (slice(None), *inner(p, half))
            sums[at] = (widen(wg[(core, *at)]) + widen(sib[at]) + widen(got1[(p, 0, *there)])).astype(BF16)
            pair_of.append(launch(sums.at[at], got1.at[(p, slot, *there)], p, i, to(p, 0, j)))
        later[p] = pair_of

    def reduce_second(p):
        for copy in (flights[p][2], flights[p][3], *later[p]):
            copy.wait_recv()
        at = (pl.ds(3 * p, 3), *pick(p, 0, 0))
        acc2[p] = widen(wg[(core, *at)]) + widen(sib[at]) + widen(got1[p, 1]) + widen(got1[p, 2])
        send2[p] = acc2[p].astype(BF16)
        flights[p] = [
            launch(send2.at[(p, slice(None), *pick(p, 1, by))], got2.at[p, i], p, 6 + i, to(p, 1, by))
            for i, by in enumerate((1, -1, 2))
        ]

    def reduce_third(p):
        for copy in flights[p]:
            copy.wait_recv()
        acc3[p] = acc2[(p, slice(None), *pick(p, 1, 0))] + widen(got2[p, 0]) + widen(got2[p, 1]) + widen(got2[p, 2])
        flights[p] = [
            launch(acc3.at[(p, slice(None), *pick(p, 2, by))], got3.at[p, i], p, 9 + i, to(p, 2, by))
            for i, by in enumerate((1, -1, 2))
        ]

    def reduce_last(p):
        for copy in flights[p]:
            copy.wait_recv()
        total[pl.ds(3 * p, 3)] = acc3[(p, slice(None), *pick(p, 2, 0))] + got3[p, 0] + got3[p, 1] + got3[p, 2]

    for n in range(4):
        lanes = pl.ds(n * 256, 256)
        value = widen(up_ref[:, lanes]) + jnp.dot(grad_two[...], by_columns(1, n), preferred_element_type=F32)
        back[:, lanes] = value
        one = value * feat[:, lanes]
        grad_one[:, lanes] = one.astype(BF16)
        bias_sum[0:1, lanes] = jnp.sum(one, axis=0, keepdims=True)
    turned_sum = bias_sum[...].T.astype(BF16).reshape(4, 4, 4, 16, 128)
    wg[0, 8] = turned_sum
    wg[1, 8] = turned_sum
    for n in range(4):
        put(0, n, outer(grad_one[:, n * 256 : n * 256 + 256], feat_bf[...]))
    share(0)
    for n in range(4):
        lanes = pl.ds(n * 256, 256)
        one = turned(feat_bf[...], by_rows(0, n)) + bias_of(0, n)
        proj[:, lanes] = one
        value = feat[:, lanes]
        layer_bf[:, lanes] = (value * one + value).astype(BF16)
    reduce_first(0)
    for n in range(4):
        put(1, n, outer(grad_two[:, n * 256 : n * 256 + 256], layer_bf[...]))
    share(1)
    share(2)
    reduce_on(0)

    def second(n):
        lanes = pl.ds(n * 256, 256)
        two = turned(layer_bf[...], by_rows(1, n)) + bias_of(1, n)
        back[:, lanes] = widen(up_ref[:, lanes]) * two + back[:, lanes] * (proj[:, lanes] + 1.0)

    def last(n):
        lanes = pl.ds(n * 256, 256)
        rest = jnp.dot(grad_one[...], by_columns(0, n), preferred_element_type=F32)
        grad_feat[:, lanes] = (back[:, lanes] + rest).astype(BF16)

    second(0)
    second(1)
    second(2)
    reduce_first(1)
    reduce_first(2)
    second(3)
    reduce_second(0)
    last(0)
    last(1)
    last(2)
    last(3)
    reduce_on(1)
    reduce_on(2)

    owner, k = iota((1024, 128), 0) >> 3, iota((1024, 128), 0) & 7
    key = jnp.where(k < 4, owner * 4 + k, jnp.where(k < 6, 512 + owner * 2 + k - 4, -1))
    key = jnp.concatenate([key] * 4, axis=1)
    summed = jnp.zeros((1024, 128), F32)
    for f in range(8):
        ids = bag_t_ref[f : f + 1, :]
        summed += jnp.dot(as_mask(key == ids), grad_feat[:, f * 128 : f * 128 + 128], preferred_element_type=F32)
        if f == 3:
            reduce_third(0)
    slots[...] = summed.reshape(64, 2, 8, 128)
    place_of = as_mask((iota((128, 128), 0) & 3) == iota((128, 128), 1))
    for a in range(4):
        number = (ids_ref[a : a + 1, :] - (a * 32 + (iota((1, 128), 1) >> 2)) * 64).astype(F32)
        row, lane = iota((256, 128), 0), iota((256, 128), 1)
        keep = ((row & 7) == 6) & ((lane >> 2) == (row >> 3))
        numbers = jnp.dot(jnp.where(keep, number, 0.0).astype(BF16), place_of, preferred_element_type=F32)
        part = pl.ds(a * 16, 16)
        slots[part] = slots[part] + numbers.reshape(16, 2, 8, 128)

    def to_chips(source, target, sem):
        def one(i, carry):
            peer = lax.rem(chip + i, 64)
            remote(source.at[peer], target.at[chip], all_send.at[sem], all_recv.at[sem], peer * 2 + core).start()
            return carry

        lax.fori_loop(1, 64, one, 0)
        target[chip] = source[chip]
        many = pl.ds(0, 63)
        return remote(source.at[many], target.at[many], all_send.at[sem], all_recv.at[sem], near)

    outward = to_chips(slots, arrived, 0)
    reduce_second(1)
    reduce_second(2)
    reduce_last(0)
    reduce_third(1)
    reduce_third(2)
    reduce_last(1)
    reduce_last(2)

    grad = total[0:8]
    fresh[...] = pair[0:8] - weight_rate * grad / (jnp.sqrt(pair[9:17] + grad * grad) + epsilon)
    bias = pair[8] - bias_rate * total[8]
    for j, t in enumerate(TILES[0]):
        buf_next[(core, j, *coords)] = fresh[t].astype(BF16)
    buf_next[(core, 4, *coords)] = bias.astype(BF16)
    following = gather_all(buf_next, GATHER_NEXT, me, core, coords, ring2_send, ring2_recv, pair2_send, pair2_recv)
    next(following)
    swap_new = remote(fresh.at[:, yours, :], other, swap_send.at[1], swap_recv.at[1], near)
    swap_new.start()
    total[8] = bias
    new_bias = total[8, mine, :]
    for layer in range(2):
        column = jnp.broadcast_to(new_bias[:, layer : layer + 1], (8, 8))
        turned_bias = jnp.where(iota((8, 8), 0) == iota((8, 8), 1), column, 0.0)
        b_new_ref[layer : layer + 1, :] = jnp.sum(turned_bias, axis=0, keepdims=True)

    outward.wait_recv()
    cross = remote(arrived.at[:, 1 - core], gathered.at[:, core], near_send.at[0], near_recv.at[0], near)
    cross.start()
    gathered[:, core] = arrived[:, core]
    next(following)
    cross.wait_recv()
    split[...] = halves_of(gathered[...].reshape(1024, 128))
    numbers = jnp.broadcast_to(gathered[:, :, 6:7, :].reshape(128, 1, 128), (128, 8, 128)).reshape(1024, 128)
    wanted = jnp.where((iota((1024, 128), 0) & 3) == iota((1024, 128), 1), numbers, 0.0)
    number = jnp.sum(wanted, axis=1, keepdims=True).astype(jnp.int32)
    lane, k = iota((1024, 128), 1), iota((1024, 128), 0) & 7
    hit = as_mask(lane == number + jnp.where(k < 4, 0, 64))
    hot_grad = joined(outer(hit, split[...]))[0:64]
    updated = accum_ref[...] + hot_grad * hot_grad
    hot_new = table_ref[...] - row_rate * hot_grad / (jnp.sqrt(updated) + epsilon)
    hot_new_ref[...] = hot_new
    hot_accum_new_ref[...] = updated
    high = hot_new.astype(BF16)
    both = jnp.concatenate([high, (hot_new - high.astype(F32)).astype(BF16)], axis=0)
    reply[...] = jnp.dot(hit, both, preferred_element_type=F32).astype(BF16).reshape(64, 2, 8, 128)
    return_near = remote(reply.at[:, 1 - core], answer.at[:, core], near_send.at[1], near_recv.at[1], near)
    return_near.start()
    answer[:, core] = reply[:, core]
    next(following)
    return_near.wait_recv()
    homeward = to_chips(answer, held, 1)
    next(following)

    bound = jnp.concatenate([dest_ref[0:1, :], dest_ref[1:2, :]], axis=1) + 1
    came_at = (iota((256, 1024), 0) & 127) * 8 + 4 + (iota((256, 1024), 0) >> 7)
    lay = as_mask(came_at == iota((256, 1024), 1))

    def laid(number):
        number = jnp.broadcast_to(number.astype(F32), (8, 256)).astype(BF16)
        return jnp.dot(number, lay, preferred_element_type=F32)[0:1]

    target = (laid(bound >> 5) * 32.0 + laid(bound & 31)).astype(jnp.int32)
    for n in range(4):
        at = pl.ds(n * 256, 256)
        hit = as_mask(iota((256, 1024), 0) + (n * 256 + 1) == target)
        owner_grad = joined(jnp.dot(hit, split[...], preferred_element_type=F32))
        updated = owner_accum_ref[at, :] + owner_grad * owner_grad
        owner_new_ref[at, :] = owner_ref[at, :] - row_rate * owner_grad / (jnp.sqrt(updated) + epsilon)
        owner_accum_new_ref[at, :] = updated
        next(following)
    bag[...] = next_t_ref[...].T

    homeward.wait_recv()
    key = (iota((1, 1024), 1) >> 3) * 4 + (iota((1, 1024), 1) & 3)
    for f in range(8):
        hit = as_mask(bag[:, f : f + 1] == key)
        value = jnp.dot(hit, held[...].reshape(1024, 128), preferred_element_type=F32)
        lanes = pl.ds(f * 128, 128)
        feat[:, lanes] = value
        feat_bf[:, lanes] = value.astype(BF16)
        if f % 2:
            next(following, None)
    for _ in following:
        pass
    for n in range(4):
        lanes = pl.ds(n * 256, 256)
        weight = jnp.concatenate([rows(buf_next[h, t, n]) for h in range(2) for t in range(4)], axis=1)
        bias = turned(as_mask(iota((8, 128), 1) == 0), rows(buf_next[0, 4, n]))[0:1]
        value = feat[:, lanes]
        out_ref[:, lanes] = (value * (turned(feat_bf[...], weight) + bias) + value).astype(BF16)
    swap_new.wait_recv()
    for layer in range(2):
        for h in range(2):
            for j, t in enumerate(TILES[layer]):
                at = h * 512 + j * 128
                w_new_ref[layer, :, at : at + 128] = jnp.where(core == h, fresh[t, mine, :], other[t])
    for copy in (swap, swap_new, cross, return_near, outward, homeward, *sends):
        copy.wait_send()


VM = pl.BlockSpec(memory_space=pltpu.VMEM)
DMA = pltpu.SemaphoreType.DMA


def local(
    upstream, bag, next_bag, hot_slots, evict_dest, hot_cache, evict_cache, hot_table, hot_accum, owner_table, owner_accum,
    cross_w, cross_b, cross_accum,
):
    wide, cube, block = (512, 1024), (9, 4, 4, 4, 16, 128), (4, 4, 16, 128)
    ring = [DMA((3, 18)), DMA((3, 18)), DMA((3, 13)), DMA((3, 13))]
    unit = (64, 2, 8, 128)
    outs = [
        (wide, BF16), ((64, 128), F32), ((64, 128), F32), ((1024, 128), F32), ((1024, 128), F32), ((2, 8, 1024), F32), ((2, 8), F32),
    ]
    scratch = [
        ((2, 17, 8, 128), F32), ((17, 16, 128), F32), ((2, *cube), BF16), ((512, 8), jnp.int32), (wide, F32), (wide, BF16),
        (wide, F32), (wide, BF16), (wide, BF16), (wide, BF16), (wide, F32), (wide, BF16), ((768, 256), BF16), ((128, 1024), F32),
        ((2, *cube), BF16), (cube, BF16), (cube, BF16), ((3, 3, 3, *block), BF16), ((3, 3, *block), F32), ((3, 3, *block), BF16),
        ((3, 3, 3, 4, 16, 128), BF16), ((3, 3, 4, 16, 128), F32), ((3, 3, 3, 16, 128), F32), ((9, 16, 128), F32),
        ((8, 16, 128), F32), ((8, 8, 128), F32), ((2, 5, *cube[1:]), BF16),
        (unit, F32), (unit, F32), (unit, F32), ((1024, 256), BF16), (unit, BF16), (unit, BF16), (unit, BF16),
    ]
    results = pl.pallas_call(
        step,
        out_shape=tuple(jax.ShapeDtypeStruct(s, d) for s, d in outs),
        in_specs=[VM] * 14,
        out_specs=tuple(VM for _ in outs),
        scratch_shapes=[
            *(pltpu.VMEM(s, d) for s, d in scratch),
            *ring, DMA((2,)), DMA((2,)), DMA((3, 12)), DMA((3, 12)), DMA((3,)), DMA((3,)), *ring,
            DMA((2,)), DMA((2,)), DMA((2,)), DMA((2,)),
        ],
        compiler_params=pltpu.CompilerParams(vmem_limit_bytes=60 * 1024 * 1024, collective_id=1, has_side_effects=True),
        cost_estimate=pl.CostEstimate(flops=12_000_000_000, bytes_accessed=12_000_000, transcendentals=0),
    )(
        jnp.swapaxes(cross_w, 1, 2), jnp.swapaxes(cross_accum, 1, 2), cross_b, bag.T, next_bag.T, hot_slots.reshape(4, 128),
        evict_dest[0].T, upstream, hot_cache, evict_cache, hot_table, hot_accum, owner_table, owner_accum,
    )
    return (*results[:5], jnp.swapaxes(results[5], 1, 2), results[6])


def solution(mesh):
    row, cube = P("dev", None), P(None, None, "dev")
    return jax.shard_map(
        local,
        mesh=mesh,
        in_specs=(row, row, row, P("dev"), P("dev", None, None), row, row, row, row, row, row, cube, P(None, "dev"), cube),
        out_specs=(row, row, row, row, row, cube, P(None, "dev")),
        check_vma=False,
    )
```

```python
import jax
import jax.numpy as jnp
from jax import lax
from jax.experimental import pallas as pl
from jax.experimental.pallas import tpu as pltpu
from jax.sharding import PartitionSpec as P

row_rate = 0.05
weight_rate = 0.005
bias_rate = 0.0002
epsilon = 1e-10

MESH = pl.DeviceIdType.MESH
F32 = jnp.float32
BF16 = jnp.bfloat16
STRIDE = (32, 8, 2)
TILES = ((0, 1, 2, 3), (5, 6, 7, 8))
BIAS = 4
GATHER = ((0, 3, (2, 1, 0)), (3, 3, (1, 0, 2)), (6, 3, (0, 2, 1)))
REDUCE = ((0, 2, (0, 1, 2)), (2, 2, (2, 0, 1)), (4, 1, (1, 2, 0)), (5, 1, (0, 1, 2)), (6, 1, (2, 0, 1)), (7, 2, (1, 2, 0)))
GATHER_NEXT = ((0, 2, (2, 1, 0)), (2, 2, (1, 0, 2)), (4, 1, (0, 2, 1)))


def place():
    me = lax.axis_index("dev")
    core = lax.rem(me, 2)
    chip = me // 2
    coords = (chip // 16, lax.rem(chip // 4, 4), lax.rem(chip, 4))
    return me, core, coords


def step_to(me, coords, axis, by):
    at = coords[axis]
    return me + (lax.rem(at + by + 4, 4) - at) * STRIDE[axis]


def sibling_of(me, core):
    return me + 1 - 2 * core


def remote(source, target, send, recv, device):
    return pltpu.make_async_remote_copy(
        src_ref=source, dst_ref=target, send_sem=send, recv_sem=recv, device_id=(device,), device_id_type=MESH
    )


def greet(me, core, coords):
    barrier = pltpu.get_barrier_semaphore()
    pl.semaphore_signal(barrier, inc=1, device_id=(sibling_of(me, core),), device_id_type=MESH)
    for axis in range(3):
        for by in (1, -1, 2):
            pl.semaphore_signal(barrier, inc=1, device_id=(step_to(me, coords, axis, by),), device_id_type=MESH)


def all_here():
    pl.semaphore_wait(pltpu.get_barrier_semaphore(), 10)


LINES = (0, -1, 1, 2)
GOES_ON = (1, 1, -1, -1)


def gather_all(buf, parts, me, core, coords, ring_send, ring_recv, pair_send, pair_recv):
    sends, pairs, count = [], [], len(parts)
    near = sibling_of(me, core)

    def move(p, index, i, device):
        first, tiles, _ = parts[p]
        ref = buf.at[(core, pl.ds(first, tiles), *index)]
        copy = remote(ref, ref, ring_send.at[p, i], ring_recv.at[p, i], device)
        copy.start()
        sends.append(copy)
        return copy

    def pass_on(p, index, i):
        first, tiles, _ = parts[p]
        ref = buf.at[(core, pl.ds(first, tiles), *index)]
        copy = remote(ref, ref, pair_send.at[p, i], pair_recv.at[p, i], near)
        copy.start()
        pairs.append(copy)

    def index(p, **at):
        order = parts[p][2]
        out = list(coords)
        out[order[0]] = pl.ds(0, 4)
        if at.get("line") is None:
            out[order[1]] = pl.ds(0, 4)
        else:
            out[order[1]] = lax.rem(coords[order[1]] + at["line"] + 4, 4)
        out[order[2]] = lax.rem(coords[order[2]] + at.get("far", 0) + 4, 4)
        return tuple(out)

    def to(p, k, by):
        return step_to(me, coords, parts[p][2][k], by)

    one = [[move(p, coords, i, to(p, 0, by)) for i, by in enumerate((1, -1, 2))] for p in range(count)]
    yield
    two, right, left, passed = [], [], [], []

    def spread(p, i):
        where = index(p, line=LINES[i])
        right[p][i] = move(p, where, 6 + i, to(p, 2, 1))
        left[p][i] = move(p, where, 10 + i, to(p, 2, -1))

    for p in range(count):
        for copy in one[p]:
            copy.wait_recv()
        where = index(p, line=0)
        two.append([move(p, where, 3 + i, to(p, 1, by)) for i, by in enumerate((1, -1, 2))])
        right.append({})
        left.append({})
        passed.append({})
        spread(p, 0)
    yield

    def arrive(p, i):
        right[p][i].wait_recv()
        if GOES_ON[i] == 1:
            passed[p][i] = move(p, index(p, line=LINES[i], far=-1), 14 + i, to(p, 2, 1))
        pass_on(p, index(p, line=LINES[i], far=-1), 1 + i)
        left[p][i].wait_recv()
        if GOES_ON[i] == -1:
            passed[p][i] = move(p, index(p, line=LINES[i], far=1), 14 + i, to(p, 2, -1))
        pass_on(p, index(p, line=LINES[i], far=1), 5 + i)

    for i in (1, 2):
        for p in range(count):
            two[p][i - 1].wait_recv()
            spread(p, i)
    yield
    for p in range(count):
        arrive(p, 0)
    yield
    for p in range(count):
        two[p][2].wait_recv()
        spread(p, 3)
        pass_on(p, index(p), 0)
    yield
    for i in (1, 2, 3):
        for p in range(count):
            arrive(p, i)
        yield
    for i in range(4):
        for p in range(count):
            passed[p][i].wait_recv()
            pass_on(p, index(p, line=LINES[i], far=2), 9 + i)
        yield
    for copy in pairs:
        copy.wait_recv()
    for copy in sends + pairs:
        copy.wait_send()


def rows(value):
    return value.reshape(-1, value.shape[-1])


def turned(a, b):
    return lax.dot_general(a, b, (((1,), (1,)), ((), ())), preferred_element_type=F32)


def outer(a, b):
    return lax.dot_general(a, b, (((0,), (0,)), ((), ())), preferred_element_type=F32)


def iota(shape, dim):
    return lax.broadcasted_iota(jnp.int32, shape, dim)


def as_mask(hit, kind=BF16):
    return jnp.where(hit, 1.0, 0.0).astype(kind)


def halves_of(value):
    high = value.astype(BF16)
    return jnp.concatenate([high, (value - high.astype(F32)).astype(BF16)], axis=1)


def joined(value):
    return value[:, 0:128] + value[:, 128:256]


def widen(value):
    return value.astype(F32)


def step(
    w_ref, a_ref, b_ref, bag_t_ref, next_t_ref, ids_ref, dest_ref, up_ref, hot_ref, evict_ref, table_ref, accum_ref, owner_ref,
    owner_accum_ref,
    out_ref, hot_new_ref, hot_accum_new_ref, owner_new_ref, owner_accum_new_ref, w_new_ref, b_new_ref,
    own, pair, buf, bag, feat, feat_bf, proj, layer_bf, grad_two, grad_one, back, grad_feat, values, bias_sum,
    wg, sib, sums, got1, acc2, send2, got2, acc3, got3, total, fresh, other, buf_next,
    slots, arrived, gathered, split, reply, answer, held,
    ring_send, ring_recv, pair_send, pair_recv, swap_send, swap_recv,
    rs_send, rs_recv, sib_send, sib_recv, ring2_send, ring2_recv, pair2_send, pair2_recv,
    all_send, all_recv, near_send, near_recv,
):
    me, core, coords = place()
    chip = me // 2
    near = sibling_of(me, core)
    mine = pl.ds(pl.multiple_of(core * 8, 8), 8)
    yours = pl.ds(pl.multiple_of(8 - core * 8, 8), 8)

    greet(me, core, coords)
    for half in range(2):
        for layer in range(2):
            for j, t in enumerate(TILES[layer]):
                lanes = pl.ds(half * 512 + j * 128, 128)
                own[half, t] = w_ref[layer, :, lanes]
                own[half, 9 + 4 * layer + j] = a_ref[layer, :, lanes]
    bias_tile = jnp.zeros((8, 128), F32)
    for layer in range(2):
        spread = jnp.where(iota((8, 8), 0) == iota((8, 8), 1), jnp.broadcast_to(b_ref[layer : layer + 1, :], (8, 8)), 0.0)
        column = jnp.sum(spread, axis=1, keepdims=True)
        bias_tile = jnp.where(iota((8, 128), 1) == layer, column, bias_tile)
    own[0, BIAS] = bias_tile
    own[1, BIAS] = bias_tile
    values[0:512] = halves_of(hot_ref[...])
    values[512:768] = halves_of(evict_ref[...])
    bag[...] = bag_t_ref[...].T
    bias_sum[...] = jnp.zeros_like(bias_sum)
    all_here()
    swap = remote(own.at[1 - core], pair.at[:, mine, :], swap_send.at[0], swap_recv.at[0], near)
    swap.start()
    pair[:, mine, :] = own[core]
    swap.wait_recv()
    buf[(core, slice(None), *coords)] = pair[0:9].astype(BF16)

    def look_up(field):
        ids = bag[:, field : field + 1]
        found = jnp.dot(as_mask(iota((512, 768), 1) == ids), values[...], preferred_element_type=F32)
        lanes = pl.ds(field * 128, 128)
        feat_bf[:, lanes] = found[:, 0:128].astype(BF16)
        value = joined(found)
        feat[:, lanes] = value
        two = widen(up_ref[:, lanes]) * value
        grad_two[:, lanes] = two.astype(BF16)
        bias_sum[1:2, lanes] = jnp.sum(two, axis=0, keepdims=True)

    field = 0
    for _ in gather_all(buf, GATHER, me, core, coords, ring_send, ring_recv, pair_send, pair_recv):
        for _ in range(2):
            if field < 8:
                look_up(field)
                field += 1

    def by_rows(layer, block):
        return jnp.concatenate([rows(buf[h, t, block]) for h in range(2) for t in TILES[layer]], axis=1)

    def by_columns(layer, block):
        picked = TILES[layer][2 * (block % 2) : 2 * (block % 2) + 2]
        return jnp.concatenate([rows(buf[block // 2, t]) for t in picked], axis=1)

    def bias_of(layer, block):
        return turned(as_mask(iota((8, 128), 1) == layer), rows(buf[0, BIAS, block]))[0:1]

    def put(layer, block, value):
        value = value.astype(BF16)
        for h in range(2):
            for j, t in enumerate(TILES[layer]):
                at = h * 512 + j * 128
                wg[h, t, block] = value[:, at : at + 128].reshape(4, 4, 16, 128)

    orders = [part[2] for part in REDUCE]
    spans = [pl.ds(part[0], part[1]) for part in REDUCE]
    sends, flights, later = [], {}, {}

    def launch(source, target, p, i, device):
        copy = remote(source, target, rs_send.at[p, i], rs_recv.at[p, i], device)
        copy.start()
        sends.append(copy)
        return copy

    def to(p, k, by):
        return step_to(me, coords, orders[p][k], by)

    def pick(p, k, j, half=None):
        order, index = orders[p], []
        for axis in sorted(order[k:]):
            if axis == order[k]:
                index.append(lax.rem(coords[axis] + j + 4, 4))
            elif half is not None and axis == order[2]:
                index.append(pl.ds(2 * half, 2))
            else:
                index.append(pl.ds(0, 4))
        return tuple(index)

    def inner(p, half):
        order = orders[p]
        return tuple(pl.ds(2 * half, 2) if axis == order[2] else pl.ds(0, 4) for axis in sorted(order[1:]))

    def share(p):
        copy = remote(wg.at[1 - core, spans[p]], sib.at[spans[p]], sib_send.at[p], sib_recv.at[p], near)
        copy.start()
        sends.append(copy)
        flights[p] = copy

    def reduce_first(p):
        flights[p].wait_recv()

        def block(j, half, slot, i, by):
            at, there = (spans[p], *pick(p, 0, j, half)), (slot, spans[p], *inner(p, half))
            sums[at] = (widen(wg[(core, *at)]) + widen(sib[at])).astype(BF16)
            return launch(sums.at[at], got1.at[there], p, i, to(p, 0, by))

        flights[p] = (block(2, 0, 0, 0, 1), block(2, 1, 0, 2, -1), block(1, 1, 1, 1, 1), block(-1, 0, 2, 3, -1))

    def reduce_on(p):
        pair_of = []
        for copy, j, half, slot, i in ((flights[p][0], 1, 0, 1, 4), (flights[p][1], -1, 1, 2, 5)):
            copy.wait_recv()
            at, there = (spans[p], *pick(p, 0, j, half)), (spans[p], *inner(p, half))
            sums[at] = (widen(wg[(core, *at)]) + widen(sib[at]) + widen(got1[(0, *there)])).astype(BF16)
            pair_of.append(launch(sums.at[at], got1.at[(slot, *there)], p, i, to(p, 0, j)))
        later[p] = pair_of

    def reduce_second(p):
        for copy in (flights[p][2], flights[p][3], *later[p]):
            copy.wait_recv()
        span, at = spans[p], (spans[p], *pick(p, 0, 0))
        acc2[span] = widen(wg[(core, *at)]) + widen(sib[at]) + widen(got1[1, span]) + widen(got1[2, span])
        send2[span] = acc2[span].astype(BF16)
        flights[p] = [
            launch(send2.at[(span, *pick(p, 1, by))], got2.at[i, span], p, 6 + i, to(p, 1, by)) for i, by in enumerate((1, -1, 2))
        ]

    def reduce_third(p):
        for copy in flights[p]:
            copy.wait_recv()
        span = spans[p]
        acc3[span] = acc2[(span, *pick(p, 1, 0))] + widen(got2[0, span]) + widen(got2[1, span]) + widen(got2[2, span])
        flights[p] = [
            launch(acc3.at[(span, *pick(p, 2, by))], got3.at[i, span], p, 9 + i, to(p, 2, by)) for i, by in enumerate((1, -1, 2))
        ]

    def reduce_last(p):
        for copy in flights[p]:
            copy.wait_recv()
        span = spans[p]
        total[span] = acc3[(span, *pick(p, 2, 0))] + got3[0, span] + got3[1, span] + got3[2, span]

    def every(stage, parts):
        for p in parts:
            stage(p)

    early, late = (0, 1, 2), (3, 4, 5)

    for n in range(4):
        lanes = pl.ds(n * 256, 256)
        value = widen(up_ref[:, lanes]) + jnp.dot(grad_two[...], by_columns(1, n), preferred_element_type=F32)
        back[:, lanes] = value
        one = value * feat[:, lanes]
        grad_one[:, lanes] = one.astype(BF16)
        bias_sum[0:1, lanes] = jnp.sum(one, axis=0, keepdims=True)
    turned_sum = bias_sum[...].T.astype(BF16).reshape(4, 4, 4, 16, 128)
    wg[0, BIAS] = turned_sum
    wg[1, BIAS] = turned_sum
    for n in range(4):
        put(0, n, outer(grad_one[:, n * 256 : n * 256 + 256], feat_bf[...]))
    every(share, early)
    for n in range(4):
        lanes = pl.ds(n * 256, 256)
        one = turned(feat_bf[...], by_rows(0, n)) + bias_of(0, n)
        proj[:, lanes] = one
        value = feat[:, lanes]
        layer_bf[:, lanes] = (value * one + value).astype(BF16)
    for n in range(4):
        put(1, n, outer(grad_two[:, n * 256 : n * 256 + 256], layer_bf[...]))
    every(share, late)
    every(reduce_first, early)

    def second(n):
        lanes = pl.ds(n * 256, 256)
        two = turned(layer_bf[...], by_rows(1, n)) + bias_of(1, n)
        back[:, lanes] = widen(up_ref[:, lanes]) * two + back[:, lanes] * (proj[:, lanes] + 1.0)

    def last(n):
        lanes = pl.ds(n * 256, 256)
        rest = jnp.dot(grad_one[...], by_columns(0, n), preferred_element_type=F32)
        grad_feat[:, lanes] = (back[:, lanes] + rest).astype(BF16)

    for n in range(4):
        second(n)
    last(0)
    last(1)
    every(reduce_on, early)
    last(2)
    last(3)

    owner, k = iota((1024, 128), 0) >> 3, iota((1024, 128), 0) & 7
    key = jnp.where(k < 4, owner * 4 + k, jnp.where(k < 6, 512 + owner * 2 + k - 4, -1))
    key = jnp.concatenate([key] * 4, axis=1)
    summed = jnp.zeros((1024, 128), F32)
    for f in range(8):
        ids = bag_t_ref[f : f + 1, :]
        summed += jnp.dot(as_mask(key == ids), grad_feat[:, f * 128 : f * 128 + 128], preferred_element_type=F32)
        if f == 3:
            every(reduce_first, late)
    every(reduce_second, early)
    slots[...] = summed.reshape(64, 2, 8, 128)
    place_of = as_mask((iota((128, 128), 0) & 3) == iota((128, 128), 1))
    for a in range(4):
        number = (ids_ref[a : a + 1, :] - (a * 32 + (iota((1, 128), 1) >> 2)) * 64).astype(F32)
        row, lane = iota((256, 128), 0), iota((256, 128), 1)
        keep = ((row & 7) == 6) & ((lane >> 2) == (row >> 3))
        numbers = jnp.dot(jnp.where(keep, number, 0.0).astype(BF16), place_of, preferred_element_type=F32)
        part = pl.ds(a * 16, 16)
        slots[part] = slots[part] + numbers.reshape(16, 2, 8, 128)

    def to_chips(source, target, sem):
        def one(i, carry):
            peer = lax.rem(chip + i, 64)
            remote(source.at[peer], target.at[chip], all_send.at[sem], all_recv.at[sem], peer * 2 + core).start()
            return carry

        lax.fori_loop(1, 64, one, 0)
        target[chip] = source[chip]
        many = pl.ds(0, 63)
        return remote(source.at[many], target.at[many], all_send.at[sem], all_recv.at[sem], near)

    outward = to_chips(slots, arrived, 0)
    every(reduce_on, late)
    every(reduce_third, early)
    every(reduce_second, late)
    every(reduce_last, early)

    def renew(layer):
        tiles = pl.ds(TILES[layer][0], 4)
        grad, squares = total[tiles], pair[9 + 4 * layer : 13 + 4 * layer]
        fresh[tiles] = pair[tiles] - weight_rate * grad / (jnp.sqrt(squares + grad * grad) + epsilon)
        copy = remote(fresh.at[tiles, yours, :], other.at[tiles], swap_send.at[1 + layer], swap_recv.at[1 + layer], near)
        copy.start()
        return copy

    renewed = renew(0)
    fresh[BIAS] = pair[BIAS] - bias_rate * total[BIAS]
    buf_next[(core, slice(None), *coords)] = fresh[0:5].astype(BF16)
    following = gather_all(buf_next, GATHER_NEXT, me, core, coords, ring2_send, ring2_recv, pair2_send, pair2_recv)
    next(following)
    new_bias = fresh[BIAS, mine, :]
    for layer in range(2):
        column = jnp.broadcast_to(new_bias[:, layer : layer + 1], (8, 8))
        turned_bias = jnp.where(iota((8, 8), 0) == iota((8, 8), 1), column, 0.0)
        b_new_ref[layer : layer + 1, :] = jnp.sum(turned_bias, axis=0, keepdims=True)

    outward.wait_recv()
    cross = remote(arrived.at[:, 1 - core], gathered.at[:, core], near_send.at[0], near_recv.at[0], near)
    cross.start()
    gathered[:, core] = arrived[:, core]
    next(following)
    cross.wait_recv()
    split[...] = halves_of(gathered[...].reshape(1024, 128))
    numbers = jnp.broadcast_to(gathered[:, :, 6:7, :].reshape(128, 1, 128), (128, 8, 128)).reshape(1024, 128)
    wanted = jnp.where((iota((1024, 128), 0) & 3) == iota((1024, 128), 1), numbers, 0.0)
    number = jnp.sum(wanted, axis=1, keepdims=True).astype(jnp.int32)
    lane, k = iota((1024, 128), 1), iota((1024, 128), 0) & 7
    hit = as_mask(lane == number + jnp.where(k < 4, 0, 64))
    hot_grad = joined(outer(hit, split[...]))[0:64]
    updated = accum_ref[...] + hot_grad * hot_grad
    hot_new = table_ref[...] - row_rate * hot_grad / (jnp.sqrt(updated) + epsilon)
    hot_new_ref[...] = hot_new
    hot_accum_new_ref[...] = updated
    high = hot_new.astype(BF16)
    both = jnp.concatenate([high, (hot_new - high.astype(F32)).astype(BF16)], axis=0)
    reply[...] = jnp.dot(hit, both, preferred_element_type=F32).astype(BF16).reshape(64, 2, 8, 128)
    return_near = remote(reply.at[:, 1 - core], answer.at[:, core], near_send.at[1], near_recv.at[1], near)
    return_near.start()
    answer[:, core] = reply[:, core]
    next(following)
    return_near.wait_recv()
    homeward = to_chips(answer, held, 1)
    next(following)
    every(reduce_third, late)

    bound = jnp.concatenate([dest_ref[0:1, :], dest_ref[1:2, :]], axis=1) + 1
    came_at = (iota((256, 1024), 0) & 127) * 8 + 4 + (iota((256, 1024), 0) >> 7)
    lay = as_mask(came_at == iota((256, 1024), 1))

    def laid(number):
        number = jnp.broadcast_to(number.astype(F32), (8, 256)).astype(BF16)
        return jnp.dot(number, lay, preferred_element_type=F32)[0:1]

    target = (laid(bound >> 5) * 32.0 + laid(bound & 31)).astype(jnp.int32)
    for n in range(4):
        at = pl.ds(n * 256, 256)
        hit = as_mask(iota((256, 1024), 0) + (n * 256 + 1) == target)
        owner_grad = joined(jnp.dot(hit, split[...], preferred_element_type=F32))
        updated = owner_accum_ref[at, :] + owner_grad * owner_grad
        owner_new_ref[at, :] = owner_ref[at, :] - row_rate * owner_grad / (jnp.sqrt(updated) + epsilon)
        owner_accum_new_ref[at, :] = updated
        next(following)
    every(reduce_last, late)
    renewed_too = renew(1)
    bag[...] = next_t_ref[...].T

    homeward.wait_recv()
    key = (iota((1, 1024), 1) >> 3) * 4 + (iota((1, 1024), 1) & 3)
    for f in range(8):
        hit = as_mask(bag[:, f : f + 1] == key)
        value = jnp.dot(hit, held[...].reshape(1024, 128), preferred_element_type=F32)
        lanes = pl.ds(f * 128, 128)
        feat[:, lanes] = value
        feat_bf[:, lanes] = value.astype(BF16)
        if f % 2:
            next(following, None)
    for _ in following:
        pass
    for n in range(4):
        lanes = pl.ds(n * 256, 256)
        weight = jnp.concatenate([rows(buf_next[h, t, n]) for h in range(2) for t in range(4)], axis=1)
        bias = turned(as_mask(iota((8, 128), 1) == 0), rows(buf_next[0, 4, n]))[0:1]
        value = feat[:, lanes]
        out_ref[:, lanes] = (value * (turned(feat_bf[...], weight) + bias) + value).astype(BF16)
    renewed.wait_recv()
    renewed_too.wait_recv()
    for layer in range(2):
        for h in range(2):
            for j, t in enumerate(TILES[layer]):
                at = h * 512 + j * 128
                w_new_ref[layer, :, at : at + 128] = jnp.where(core == h, fresh[t, mine, :], other[t])
    for copy in (swap, renewed, renewed_too, cross, return_near, outward, homeward, *sends):
        copy.wait_send()


def keep(*refs):
    count = (len(refs) - 2) // 3
    came, gone = refs[-2:]
    loads = [pltpu.make_async_copy(refs[i], refs[2 * count + i], came.at[i]) for i in range(count)]
    stores = [pltpu.make_async_copy(refs[2 * count + i], refs[count + i], gone.at[i]) for i in range(count)]
    for copy in loads:
        copy.start()
    for load, store in zip(loads, stores):
        load.wait()
        store.start()
    for copy in stores:
        copy.wait()


VM = pl.BlockSpec(memory_space=pltpu.VMEM)
ANY = pl.BlockSpec(memory_space=pl.ANY)
DMA = pltpu.SemaphoreType.DMA


def local(
    upstream, bag, next_bag, hot_slots, evict_dest, hot_cache, evict_cache, hot_table, hot_accum, owner_table, owner_accum,
    cross_w, cross_b, cross_accum,
):
    wide, cube, block = (512, 1024), (9, 4, 4, 4, 16, 128), (4, 4, 16, 128)
    ring = [DMA((3, 18)), DMA((3, 18)), DMA((3, 13)), DMA((3, 13))]
    unit = (64, 2, 8, 128)
    outs = [
        (wide, BF16), ((64, 128), F32), ((64, 128), F32), ((1024, 128), F32), ((1024, 128), F32), ((2, 8, 1024), F32), ((2, 8), F32),
    ]
    scratch = [
        ((2, 17, 8, 128), F32), ((17, 16, 128), F32), ((2, *cube), BF16), ((512, 8), jnp.int32), (wide, F32), (wide, BF16),
        (wide, F32), (wide, BF16), (wide, BF16), (wide, BF16), (wide, F32), (wide, BF16), ((768, 256), BF16), ((128, 1024), F32),
        ((2, *cube), BF16), (cube, BF16), (cube, BF16), ((3, 9, *block), BF16), ((9, *block), F32), ((9, *block), BF16),
        ((3, 9, 4, 16, 128), BF16), ((9, 4, 16, 128), F32), ((3, 9, 16, 128), F32), ((9, 16, 128), F32),
        ((9, 16, 128), F32), ((9, 8, 128), F32), ((2, 5, *cube[1:]), BF16),
        (unit, F32), (unit, F32), (unit, F32), ((1024, 256), BF16), (unit, BF16), (unit, BF16), (unit, BF16),
    ]
    results = pl.pallas_call(
        step,
        out_shape=tuple(jax.ShapeDtypeStruct(s, d) for s, d in outs),
        in_specs=[VM] * 14,
        out_specs=tuple(VM for _ in outs),
        scratch_shapes=[
            *(pltpu.VMEM(s, d) for s, d in scratch),
            *ring, DMA((3,)), DMA((3,)), DMA((6, 12)), DMA((6, 12)), DMA((6,)), DMA((6,)), *ring,
            DMA((2,)), DMA((2,)), DMA((2,)), DMA((2,)),
        ],
        compiler_params=pltpu.CompilerParams(vmem_limit_bytes=60 * 1024 * 1024, collective_id=1, has_side_effects=True),
        cost_estimate=pl.CostEstimate(flops=12_000_000_000, bytes_accessed=12_000_000, transcendentals=0),
    )(
        jnp.swapaxes(cross_w, 1, 2), jnp.swapaxes(cross_accum, 1, 2), cross_b, bag.T, next_bag.T, hot_slots.reshape(4, 128),
        evict_dest[0].T, upstream, hot_cache, evict_cache, hot_table, hot_accum, owner_table, owner_accum,
    )
    results = pl.pallas_call(
        keep,
        out_shape=tuple(jax.ShapeDtypeStruct(s, d) for s, d in outs),
        in_specs=[ANY] * len(outs),
        out_specs=tuple(ANY for _ in outs),
        scratch_shapes=[*(pltpu.VMEM(s, d) for s, d in outs), DMA((len(outs),)), DMA((len(outs),))],
    )(*results)
    return (*results[:5], jnp.swapaxes(results[5], 1, 2), results[6])


def solution(mesh):
    row, cube = P("dev", None), P(None, None, "dev")
    return jax.shard_map(
        local,
        mesh=mesh,
        in_specs=(row, row, row, P("dev"), P("dev", None, None), row, row, row, row, row, row, cube, P(None, "dev"), cube),
        out_specs=(row, row, row, row, row, cube, P(None, "dev")),
        check_vma=False,
    )
```

```python
import jax
import jax.numpy as jnp
from jax import lax
from jax.experimental import pallas as pl
from jax.experimental.pallas import tpu as pltpu
from jax.sharding import PartitionSpec as P

row_rate = 0.05
weight_rate = 0.005
bias_rate = 0.0002
epsilon = 1e-10

MESH = pl.DeviceIdType.MESH
F32 = jnp.float32
BF16 = jnp.bfloat16
STRIDE = (32, 8, 2)
TILES = ((0, 1, 2, 3), (5, 6, 7, 8))
BIAS = 4
GATHER = ((0, 3, (2, 1, 0)), (3, 3, (1, 0, 2)), (6, 3, (0, 2, 1)))
REDUCE = ((0, 2, (0, 1, 2)), (2, 2, (2, 0, 1)), (4, 1, (1, 2, 0)), (5, 1, (0, 1, 2)), (6, 1, (2, 0, 1)), (7, 2, (1, 2, 0)))
GATHER_NEXT = ((0, 2, (2, 1, 0)), (2, 2, (1, 0, 2)), (4, 1, (0, 2, 1)))


def place():
    me = lax.axis_index("dev")
    core = lax.rem(me, 2)
    chip = me // 2
    coords = (chip // 16, lax.rem(chip // 4, 4), lax.rem(chip, 4))
    return me, core, coords


def step_to(me, coords, axis, by):
    at = coords[axis]
    return me + (lax.rem(at + by + 4, 4) - at) * STRIDE[axis]


def sibling_of(me, core):
    return me + 1 - 2 * core


def remote(source, target, send, recv, device):
    return pltpu.make_async_remote_copy(
        src_ref=source, dst_ref=target, send_sem=send, recv_sem=recv, device_id=(device,), device_id_type=MESH
    )


def greet(me, core, coords):
    barrier = pltpu.get_barrier_semaphore()
    pl.semaphore_signal(barrier, inc=1, device_id=(sibling_of(me, core),), device_id_type=MESH)
    for axis in range(3):
        for by in (1, -1, 2):
            pl.semaphore_signal(barrier, inc=1, device_id=(step_to(me, coords, axis, by),), device_id_type=MESH)


def all_here():
    pl.semaphore_wait(pltpu.get_barrier_semaphore(), 10)


LINES = (0, -1, 1, 2)
GOES_ON = (1, 1, -1, -1)


def gather_all(buf, parts, me, core, coords, ring_send, ring_recv, pair_send, pair_recv):
    sends, pairs, count = [], [], len(parts)
    near = sibling_of(me, core)

    def move(p, index, i, device):
        first, tiles, _ = parts[p]
        ref = buf.at[(core, pl.ds(first, tiles), *index)]
        copy = remote(ref, ref, ring_send.at[p, i], ring_recv.at[p, i], device)
        copy.start()
        sends.append(copy)
        return copy

    def pass_on(p, index, i):
        first, tiles, _ = parts[p]
        ref = buf.at[(core, pl.ds(first, tiles), *index)]
        copy = remote(ref, ref, pair_send.at[p, i], pair_recv.at[p, i], near)
        copy.start()
        pairs.append(copy)

    def index(p, **at):
        order = parts[p][2]
        out = list(coords)
        out[order[0]] = pl.ds(0, 4)
        if at.get("line") is None:
            out[order[1]] = pl.ds(0, 4)
        else:
            out[order[1]] = lax.rem(coords[order[1]] + at["line"] + 4, 4)
        out[order[2]] = lax.rem(coords[order[2]] + at.get("far", 0) + 4, 4)
        return tuple(out)

    def to(p, k, by):
        return step_to(me, coords, parts[p][2][k], by)

    one = [[move(p, coords, i, to(p, 0, by)) for i, by in enumerate((1, -1, 2))] for p in range(count)]
    yield
    two, right, left, passed = [], [], [], []

    def spread(p, i):
        where = index(p, line=LINES[i])
        right[p][i] = move(p, where, 6 + i, to(p, 2, 1))
        left[p][i] = move(p, where, 10 + i, to(p, 2, -1))

    for p in range(count):
        for copy in one[p]:
            copy.wait_recv()
        where = index(p, line=0)
        two.append([move(p, where, 3 + i, to(p, 1, by)) for i, by in enumerate((1, -1, 2))])
        right.append({})
        left.append({})
        passed.append({})
        spread(p, 0)
    yield

    def arrive(p, i):
        right[p][i].wait_recv()
        if GOES_ON[i] == 1:
            passed[p][i] = move(p, index(p, line=LINES[i], far=-1), 14 + i, to(p, 2, 1))
        pass_on(p, index(p, line=LINES[i], far=-1), 1 + i)
        left[p][i].wait_recv()
        if GOES_ON[i] == -1:
            passed[p][i] = move(p, index(p, line=LINES[i], far=1), 14 + i, to(p, 2, -1))
        pass_on(p, index(p, line=LINES[i], far=1), 5 + i)

    for i in (1, 2):
        for p in range(count):
            two[p][i - 1].wait_recv()
            spread(p, i)
    yield
    for p in range(count):
        arrive(p, 0)
    yield
    for p in range(count):
        two[p][2].wait_recv()
        spread(p, 3)
        pass_on(p, index(p), 0)
    yield
    for i in (1, 2, 3):
        for p in range(count):
            arrive(p, i)
        yield
    for i in range(4):
        for p in range(count):
            passed[p][i].wait_recv()
            pass_on(p, index(p, line=LINES[i], far=2), 9 + i)
        yield
    for copy in pairs:
        copy.wait_recv()
    for copy in sends + pairs:
        copy.wait_send()


def rows(value):
    return value.reshape(-1, value.shape[-1])


def turned(a, b):
    return lax.dot_general(a, b, (((1,), (1,)), ((), ())), preferred_element_type=F32)


def outer(a, b):
    return lax.dot_general(a, b, (((0,), (0,)), ((), ())), preferred_element_type=F32)


def iota(shape, dim):
    return lax.broadcasted_iota(jnp.int32, shape, dim)


def as_mask(hit, kind=BF16):
    return jnp.where(hit, 1.0, 0.0).astype(kind)


def halves_of(value):
    high = value.astype(BF16)
    return jnp.concatenate([high, (value - high.astype(F32)).astype(BF16)], axis=1)


def joined(value):
    return value[:, 0:128] + value[:, 128:256]


def widen(value):
    return value.astype(F32)


def step(
    w_ref, a_ref, b_ref, bag_t_ref, next_t_ref, ids_ref, dest_ref, up_ref, hot_ref, evict_ref, table_ref, accum_ref, owner_ref,
    owner_accum_ref,
    out_ref, hot_new_ref, hot_accum_new_ref, owner_new_ref, owner_accum_new_ref, w_new_ref, b_new_ref,
    own, pair, buf, bag, feat, feat_bf, proj, layer_bf, grad_two, grad_one, back, grad_feat, values, bias_sum,
    wg, sib, sums, got1, acc2, send2, got2, acc3, got3, total, fresh, other, buf_next,
    slots, arrived, gathered, split, reply, answer, held,
    ring_send, ring_recv, pair_send, pair_recv, swap_send, swap_recv,
    rs_send, rs_recv, sib_send, sib_recv, ring2_send, ring2_recv, pair2_send, pair2_recv,
    all_send, all_recv, near_send, near_recv,
):
    me, core, coords = place()
    chip = me // 2
    near = sibling_of(me, core)
    mine = pl.ds(pl.multiple_of(core * 8, 8), 8)
    yours = pl.ds(pl.multiple_of(8 - core * 8, 8), 8)

    greet(me, core, coords)
    for half in range(2):
        for layer in range(2):
            for j, t in enumerate(TILES[layer]):
                lanes = pl.ds(half * 512 + j * 128, 128)
                own[half, t] = w_ref[layer, :, lanes]
                own[half, 9 + 4 * layer + j] = a_ref[layer, :, lanes]
    bias_tile = jnp.zeros((8, 128), F32)
    for layer in range(2):
        spread = jnp.where(iota((8, 8), 0) == iota((8, 8), 1), jnp.broadcast_to(b_ref[layer : layer + 1, :], (8, 8)), 0.0)
        column = jnp.sum(spread, axis=1, keepdims=True)
        bias_tile = jnp.where(iota((8, 128), 1) == layer, column, bias_tile)
    own[0, BIAS] = bias_tile
    own[1, BIAS] = bias_tile
    values[0:512] = halves_of(hot_ref[...])
    values[512:768] = halves_of(evict_ref[...])
    bag[...] = bag_t_ref[...].T
    bias_sum[...] = jnp.zeros_like(bias_sum)
    all_here()
    swap = remote(own.at[1 - core], pair.at[:, mine, :], swap_send.at[0], swap_recv.at[0], near)
    swap.start()
    pair[:, mine, :] = own[core]
    swap.wait_recv()
    buf[(core, slice(None), *coords)] = pair[0:9].astype(BF16)

    def look_up(field):
        ids = bag[:, field : field + 1]
        found = jnp.dot(as_mask(iota((512, 768), 1) == ids), values[...], preferred_element_type=F32)
        lanes = pl.ds(field * 128, 128)
        feat_bf[:, lanes] = found[:, 0:128].astype(BF16)
        value = joined(found)
        feat[:, lanes] = value
        two = widen(up_ref[:, lanes]) * value
        grad_two[:, lanes] = two.astype(BF16)
        bias_sum[1:2, lanes] = jnp.sum(two, axis=0, keepdims=True)

    field = 0
    for turn, _ in enumerate(gather_all(buf, GATHER, me, core, coords, ring_send, ring_recv, pair_send, pair_recv)):
        for _ in range((3, 3, 1, 1)[min(turn, 3)]):
            if field < 8:
                look_up(field)
                field += 1

    def by_rows(layer, block):
        return jnp.concatenate([rows(buf[h, t, block]) for h in range(2) for t in TILES[layer]], axis=1)

    def by_columns(layer, block):
        picked = TILES[layer][2 * (block % 2) : 2 * (block % 2) + 2]
        return jnp.concatenate([rows(buf[block // 2, t]) for t in picked], axis=1)

    def bias_of(layer, block):
        return turned(as_mask(iota((8, 128), 1) == layer), rows(buf[0, BIAS, block]))[0:1]

    def put(layer, block, value):
        value = value.astype(BF16)
        for h in range(2):
            for j, t in enumerate(TILES[layer]):
                at = h * 512 + j * 128
                wg[h, t, block] = value[:, at : at + 128].reshape(4, 4, 16, 128)

    orders = [part[2] for part in REDUCE]
    spans = [pl.ds(part[0], part[1]) for part in REDUCE]
    sends, flights, later = [], {}, {}

    def launch(source, target, p, i, device):
        copy = remote(source, target, rs_send.at[p, i], rs_recv.at[p, i], device)
        copy.start()
        sends.append(copy)
        return copy

    def to(p, k, by):
        return step_to(me, coords, orders[p][k], by)

    def pick(p, k, j, half=None):
        order, index = orders[p], []
        for axis in sorted(order[k:]):
            if axis == order[k]:
                index.append(lax.rem(coords[axis] + j + 4, 4))
            elif half is not None and axis == order[2]:
                index.append(pl.ds(2 * half, 2))
            else:
                index.append(pl.ds(0, 4))
        return tuple(index)

    def inner(p, half):
        order = orders[p]
        return tuple(pl.ds(2 * half, 2) if axis == order[2] else pl.ds(0, 4) for axis in sorted(order[1:]))

    def share(p):
        copy = remote(wg.at[1 - core, spans[p]], sib.at[spans[p]], sib_send.at[p], sib_recv.at[p], near)
        copy.start()
        sends.append(copy)
        flights[p] = copy

    def reduce_first(p):
        flights[p].wait_recv()

        def block(j, half, slot, i, by):
            at, there = (spans[p], *pick(p, 0, j, half)), (slot, spans[p], *inner(p, half))
            sums[at] = (widen(wg[(core, *at)]) + widen(sib[at])).astype(BF16)
            return launch(sums.at[at], got1.at[there], p, i, to(p, 0, by))

        flights[p] = (block(2, 0, 0, 0, 1), block(2, 1, 0, 2, -1), block(1, 1, 1, 1, 1), block(-1, 0, 2, 3, -1))

    def reduce_on(p):
        pair_of = []
        for copy, j, half, slot, i in ((flights[p][0], 1, 0, 1, 4), (flights[p][1], -1, 1, 2, 5)):
            copy.wait_recv()
            at, there = (spans[p], *pick(p, 0, j, half)), (spans[p], *inner(p, half))
            sums[at] = (widen(wg[(core, *at)]) + widen(sib[at]) + widen(got1[(0, *there)])).astype(BF16)
            pair_of.append(launch(sums.at[at], got1.at[(slot, *there)], p, i, to(p, 0, j)))
        later[p] = pair_of

    def reduce_second(p):
        for copy in (flights[p][2], flights[p][3], *later[p]):
            copy.wait_recv()
        span, at = spans[p], (spans[p], *pick(p, 0, 0))
        acc2[span] = widen(wg[(core, *at)]) + widen(sib[at]) + widen(got1[1, span]) + widen(got1[2, span])
        send2[span] = acc2[span].astype(BF16)
        flights[p] = [
            launch(send2.at[(span, *pick(p, 1, by))], got2.at[i, span], p, 6 + i, to(p, 1, by)) for i, by in enumerate((1, -1, 2))
        ]

    def reduce_third(p):
        for copy in flights[p]:
            copy.wait_recv()
        span = spans[p]
        acc3[span] = acc2[(span, *pick(p, 1, 0))] + widen(got2[0, span]) + widen(got2[1, span]) + widen(got2[2, span])
        flights[p] = [
            launch(acc3.at[(span, *pick(p, 2, by))], got3.at[i, span], p, 9 + i, to(p, 2, by)) for i, by in enumerate((1, -1, 2))
        ]

    def reduce_last(p):
        for copy in flights[p]:
            copy.wait_recv()
        span = spans[p]
        total[span] = acc3[(span, *pick(p, 2, 0))] + got3[0, span] + got3[1, span] + got3[2, span]

    def every(stage, parts):
        for p in parts:
            stage(p)

    early, late = (0, 1, 2), (3, 4, 5)

    for n in range(4):
        lanes = pl.ds(n * 256, 256)
        value = widen(up_ref[:, lanes]) + jnp.dot(grad_two[...], by_columns(1, n), preferred_element_type=F32)
        back[:, lanes] = value
        one = value * feat[:, lanes]
        grad_one[:, lanes] = one.astype(BF16)
        bias_sum[0:1, lanes] = jnp.sum(one, axis=0, keepdims=True)
    turned_sum = bias_sum[...].T.astype(BF16).reshape(4, 4, 4, 16, 128)
    wg[0, BIAS] = turned_sum
    wg[1, BIAS] = turned_sum
    for n in range(4):
        put(0, n, outer(grad_one[:, n * 256 : n * 256 + 256], feat_bf[...]))
    every(share, early)
    for n in range(4):
        lanes = pl.ds(n * 256, 256)
        one = turned(feat_bf[...], by_rows(0, n)) + bias_of(0, n)
        proj[:, lanes] = one
        value = feat[:, lanes]
        layer_bf[:, lanes] = (value * one + value).astype(BF16)
    for n in range(4):
        put(1, n, outer(grad_two[:, n * 256 : n * 256 + 256], layer_bf[...]))
    every(share, late)
    every(reduce_first, early)

    def second(n):
        lanes = pl.ds(n * 256, 256)
        two = turned(layer_bf[...], by_rows(1, n)) + bias_of(1, n)
        back[:, lanes] = widen(up_ref[:, lanes]) * two + back[:, lanes] * (proj[:, lanes] + 1.0)

    def last(n):
        lanes = pl.ds(n * 256, 256)
        rest = jnp.dot(grad_one[...], by_columns(0, n), preferred_element_type=F32)
        grad_feat[:, lanes] = (back[:, lanes] + rest).astype(BF16)

    for n in range(4):
        second(n)
    last(0)
    last(1)
    every(reduce_on, early)
    last(2)
    last(3)

    owner, k = iota((1024, 128), 0) >> 3, iota((1024, 128), 0) & 7
    key = jnp.where(k < 4, owner * 4 + k, jnp.where(k < 6, 512 + owner * 2 + k - 4, -1))
    key = jnp.concatenate([key] * 4, axis=1)
    summed = jnp.zeros((1024, 128), F32)
    for f in range(8):
        ids = bag_t_ref[f : f + 1, :]
        summed += jnp.dot(as_mask(key == ids), grad_feat[:, f * 128 : f * 128 + 128], preferred_element_type=F32)
        if f == 3:
            every(reduce_first, late)
    every(reduce_second, early)
    slots[...] = summed.reshape(64, 2, 8, 128)
    place_of = as_mask((iota((128, 128), 0) & 3) == iota((128, 128), 1))
    for a in range(4):
        number = (ids_ref[a : a + 1, :] - (a * 32 + (iota((1, 128), 1) >> 2)) * 64).astype(F32)
        row, lane = iota((256, 128), 0), iota((256, 128), 1)
        keep = ((row & 7) == 6) & ((lane >> 2) == (row >> 3))
        numbers = jnp.dot(jnp.where(keep, number, 0.0).astype(BF16), place_of, preferred_element_type=F32)
        part = pl.ds(a * 16, 16)
        slots[part] = slots[part] + numbers.reshape(16, 2, 8, 128)

    def to_chips(source, target, sem):
        def one(i, carry):
            peer = lax.rem(chip + i, 64)
            remote(source.at[peer], target.at[chip], all_send.at[sem], all_recv.at[sem], peer * 2 + core).start()
            return carry

        lax.fori_loop(1, 64, one, 0)
        target[chip] = source[chip]
        many = pl.ds(0, 63)
        return remote(source.at[many], target.at[many], all_send.at[sem], all_recv.at[sem], near)

    outward = to_chips(slots, arrived, 0)
    every(reduce_on, late)
    every(reduce_third, early)
    every(reduce_second, late)
    every(reduce_last, early)

    def renew(layer):
        tiles = pl.ds(TILES[layer][0], 4)
        grad, squares = total[tiles], pair[9 + 4 * layer : 13 + 4 * layer]
        fresh[tiles] = pair[tiles] - weight_rate * grad / (jnp.sqrt(squares + grad * grad) + epsilon)
        copy = remote(fresh.at[tiles, yours, :], other.at[tiles], swap_send.at[1 + layer], swap_recv.at[1 + layer], near)
        copy.start()
        return copy

    renewed = renew(0)
    fresh[BIAS] = pair[BIAS] - bias_rate * total[BIAS]
    buf_next[(core, slice(None), *coords)] = fresh[0:5].astype(BF16)
    following = gather_all(buf_next, GATHER_NEXT, me, core, coords, ring2_send, ring2_recv, pair2_send, pair2_recv)
    next(following)
    new_bias = fresh[BIAS, mine, :]
    for layer in range(2):
        column = jnp.broadcast_to(new_bias[:, layer : layer + 1], (8, 8))
        turned_bias = jnp.where(iota((8, 8), 0) == iota((8, 8), 1), column, 0.0)
        b_new_ref[layer : layer + 1, :] = jnp.sum(turned_bias, axis=0, keepdims=True)

    outward.wait_recv()
    cross = remote(arrived.at[:, 1 - core], gathered.at[:, core], near_send.at[0], near_recv.at[0], near)
    cross.start()
    gathered[:, core] = arrived[:, core]
    next(following)
    cross.wait_recv()
    split[...] = halves_of(gathered[...].reshape(1024, 128))
    numbers = jnp.broadcast_to(gathered[:, :, 6:7, :].reshape(128, 1, 128), (128, 8, 128)).reshape(1024, 128)
    wanted = jnp.where((iota((1024, 128), 0) & 3) == iota((1024, 128), 1), numbers, 0.0)
    number = jnp.sum(wanted, axis=1, keepdims=True).astype(jnp.int32)
    lane, k = iota((1024, 128), 1), iota((1024, 128), 0) & 7
    hit = as_mask(lane == number + jnp.where(k < 4, 0, 64))
    hot_grad = joined(outer(hit, split[...]))[0:64]
    updated = accum_ref[...] + hot_grad * hot_grad
    hot_new = table_ref[...] - row_rate * hot_grad / (jnp.sqrt(updated) + epsilon)
    hot_new_ref[...] = hot_new
    hot_accum_new_ref[...] = updated
    high = hot_new.astype(BF16)
    both = jnp.concatenate([high, (hot_new - high.astype(F32)).astype(BF16)], axis=0)
    reply[...] = jnp.dot(hit, both, preferred_element_type=F32).astype(BF16).reshape(64, 2, 8, 128)
    return_near = remote(reply.at[:, 1 - core], answer.at[:, core], near_send.at[1], near_recv.at[1], near)
    return_near.start()
    answer[:, core] = reply[:, core]
    next(following)
    return_near.wait_recv()
    homeward = to_chips(answer, held, 1)
    next(following)
    every(reduce_third, late)

    bound = jnp.concatenate([dest_ref[0:1, :], dest_ref[1:2, :]], axis=1) + 1
    came_at = (iota((256, 1024), 0) & 127) * 8 + 4 + (iota((256, 1024), 0) >> 7)
    lay = as_mask(came_at == iota((256, 1024), 1))

    def laid(number):
        number = jnp.broadcast_to(number.astype(F32), (8, 256)).astype(BF16)
        return jnp.dot(number, lay, preferred_element_type=F32)[0:1]

    target = (laid(bound >> 5) * 32.0 + laid(bound & 31)).astype(jnp.int32)
    for n in range(4):
        at = pl.ds(n * 256, 256)
        hit = as_mask(iota((256, 1024), 0) + (n * 256 + 1) == target)
        owner_grad = joined(jnp.dot(hit, split[...], preferred_element_type=F32))
        updated = owner_accum_ref[at, :] + owner_grad * owner_grad
        owner_new_ref[at, :] = owner_ref[at, :] - row_rate * owner_grad / (jnp.sqrt(updated) + epsilon)
        owner_accum_new_ref[at, :] = updated
        next(following)
    bag[...] = next_t_ref[...].T

    homeward.wait_recv()
    key = (iota((1, 1024), 1) >> 3) * 4 + (iota((1, 1024), 1) & 3)
    for f in range(8):
        hit = as_mask(bag[:, f : f + 1] == key)
        value = jnp.dot(hit, held[...].reshape(1024, 128), preferred_element_type=F32)
        lanes = pl.ds(f * 128, 128)
        feat[:, lanes] = value
        feat_bf[:, lanes] = value.astype(BF16)
        if f % 2:
            next(following, None)
    for _ in following:
        pass
    every(reduce_last, late)
    renewed_too = renew(1)
    for n in range(4):
        lanes = pl.ds(n * 256, 256)
        weight = jnp.concatenate([rows(buf_next[h, t, n]) for h in range(2) for t in range(4)], axis=1)
        bias = turned(as_mask(iota((8, 128), 1) == 0), rows(buf_next[0, 4, n]))[0:1]
        value = feat[:, lanes]
        out_ref[:, lanes] = (value * (turned(feat_bf[...], weight) + bias) + value).astype(BF16)
    renewed.wait_recv()
    renewed_too.wait_recv()
    for layer in range(2):
        for h in range(2):
            for j, t in enumerate(TILES[layer]):
                at = h * 512 + j * 128
                w_new_ref[layer, :, at : at + 128] = jnp.where(core == h, fresh[t, mine, :], other[t])
    for copy in (swap, renewed, renewed_too, cross, return_near, outward, homeward, *sends):
        copy.wait_send()


def keep(*refs):
    count = (len(refs) - 2) // 3
    came, gone = refs[-2:]
    loads = [pltpu.make_async_copy(refs[i], refs[2 * count + i], came.at[i]) for i in range(count)]
    stores = [pltpu.make_async_copy(refs[2 * count + i], refs[count + i], gone.at[i]) for i in range(count)]
    for copy in loads:
        copy.start()
    for load, store in zip(loads, stores):
        load.wait()
        store.start()
    for copy in stores:
        copy.wait()


VM = pl.BlockSpec(memory_space=pltpu.VMEM)
ANY = pl.BlockSpec(memory_space=pl.ANY)
DMA = pltpu.SemaphoreType.DMA


def local(
    upstream, bag, next_bag, hot_slots, evict_dest, hot_cache, evict_cache, hot_table, hot_accum, owner_table, owner_accum,
    cross_w, cross_b, cross_accum,
):
    wide, cube, block = (512, 1024), (9, 4, 4, 4, 16, 128), (4, 4, 16, 128)
    ring = [DMA((3, 18)), DMA((3, 18)), DMA((3, 13)), DMA((3, 13))]
    unit = (64, 2, 8, 128)
    outs = [
        (wide, BF16), ((64, 128), F32), ((64, 128), F32), ((1024, 128), F32), ((1024, 128), F32), ((2, 8, 1024), F32), ((2, 8), F32),
    ]
    scratch = [
        ((2, 17, 8, 128), F32), ((17, 16, 128), F32), ((2, *cube), BF16), ((512, 8), jnp.int32), (wide, F32), (wide, BF16),
        (wide, F32), (wide, BF16), (wide, BF16), (wide, BF16), (wide, F32), (wide, BF16), ((768, 256), BF16), ((128, 1024), F32),
        ((2, *cube), BF16), (cube, BF16), (cube, BF16), ((3, 9, *block), BF16), ((9, *block), F32), ((9, *block), BF16),
        ((3, 9, 4, 16, 128), BF16), ((9, 4, 16, 128), F32), ((3, 9, 16, 128), F32), ((9, 16, 128), F32),
        ((9, 16, 128), F32), ((9, 8, 128), F32), ((2, 5, *cube[1:]), BF16),
        (unit, F32), (unit, F32), (unit, F32), ((1024, 256), BF16), (unit, BF16), (unit, BF16), (unit, BF16),
    ]
    results = pl.pallas_call(
        step,
        out_shape=tuple(jax.ShapeDtypeStruct(s, d) for s, d in outs),
        in_specs=[VM] * 14,
        out_specs=tuple(VM for _ in outs),
        scratch_shapes=[
            *(pltpu.VMEM(s, d) for s, d in scratch),
            *ring, DMA((3,)), DMA((3,)), DMA((6, 12)), DMA((6, 12)), DMA((6,)), DMA((6,)), *ring,
            DMA((2,)), DMA((2,)), DMA((2,)), DMA((2,)),
        ],
        compiler_params=pltpu.CompilerParams(vmem_limit_bytes=60 * 1024 * 1024, collective_id=1, has_side_effects=True),
        cost_estimate=pl.CostEstimate(flops=12_000_000_000, bytes_accessed=12_000_000, transcendentals=0),
    )(
        jnp.swapaxes(cross_w, 1, 2), jnp.swapaxes(cross_accum, 1, 2), cross_b, bag.T, next_bag.T, hot_slots.reshape(4, 128),
        evict_dest[0].T, upstream, hot_cache, evict_cache, hot_table, hot_accum, owner_table, owner_accum,
    )
    results = pl.pallas_call(
        keep,
        out_shape=tuple(jax.ShapeDtypeStruct(s, d) for s, d in outs),
        in_specs=[ANY] * len(outs),
        out_specs=tuple(ANY for _ in outs),
        scratch_shapes=[*(pltpu.VMEM(s, d) for s, d in outs), DMA((len(outs),)), DMA((len(outs),))],
    )(*results)
    return (*results[:5], jnp.swapaxes(results[5], 1, 2), results[6])


def solution(mesh):
    row, cube = P("dev", None), P(None, None, "dev")
    return jax.shard_map(
        local,
        mesh=mesh,
        in_specs=(row, row, row, P("dev"), P("dev", None, None), row, row, row, row, row, row, cube, P(None, "dev"), cube),
        out_specs=(row, row, row, row, row, cube, P(None, "dev")),
        check_vma=False,
    )
```
